512 devices in a mesh: lat: 16 (over z_hi, x), lon: 32 (over z_lo, y, core).
Axes of the slice: x: 4, y: 4, z: 16 (z_hi: 4, z_lo: 4; z = z_hi * 4 + z_lo), core: 2. Of those that a mesh axis runs over, the one named last changes fastest.
Arguments:
- state_field: bfloat16 [128, 1024, 256], P('lat', 'lon'), may hold values from -6 to 6
- support_offsets: int32 [128, 5, 8], replicated, may hold values from -8 to 8, as said below
- kernel_values: bfloat16 [3, 128, 5, 8], replicated, may hold values from -1 to 1
- basis_weight: bfloat16 [3, 256, 256], replicated, may hold values from -0.21875 to 0.21875
- weight_in: bfloat16 [256, 1024], replicated, may hold values from -0.375 to 0.375
- weight_out: bfloat16 [1024, 256], replicated, may hold values from -0.1875 to 0.1875
- cotangent: bfloat16 [128, 1024, 256], P('lat', 'lon'), may hold values from -6 to 6
Outputs:
- block_out: bfloat16 [128, 1024, 256], P('lat', 'lon')
- grad_field: bfloat16 [128, 1024, 256], P('lat', 'lon')
- grad_basis_weight: bfloat16 [3, 256, 256], replicated
- grad_weight_in: bfloat16 [256, 1024], replicated
- grad_weight_out: bfloat16 [1024, 256], replicated
The draws below stay inside these ranges and needn't reach their ends.
Inputs may be any that keep to these rules, and one draw needn't show every extreme that they name: `support_offsets`: with p = min(i, 127 - i) and w(i) = max(1, 8 // (1 + p // 8)), every offset of cycle i lies within -w(i)..w(i); slot 0 holds w(i) and slot 1 holds -w(i) for every cycle and latitude offset.
All inputs are finite; a program needn't handle non-finite values.
Results may differ from the reference program's by a relative error of at most 0.017.
Values may be sent and summed in bfloat16 or wider, within the bound.
No kernel may reach another device: no remote copies, remote signals or barrier semaphores. Data moves between devices by JAX's collectives and lax.ppermute only.
A program may use at most 64 MiB of HBM per device.

```python
import math
import jax
import jax.numpy as jnp
from jax import lax

C = 256
FF = 1024
K = 3
RAD = 2
WIDE = 8
SLOTS = 8
LAT_DEV = 8
NLAT = 128
NLON = 1024


def draw_support_offsets(key, part):
    key = jax.random.fold_in(key, 7)
    cycle_ids = jnp.arange(NLAT, dtype=jnp.int32)
    polar = jnp.minimum(cycle_ids, NLAT - 1 - cycle_ids)
    reach = jnp.maximum(1, WIDE // (1 + polar // LAT_DEV))
    raw_bits = jax.random.randint(key, (NLAT, 2 * RAD + 1, SLOTS), 0, 1 << 20, dtype=jnp.int32)
    spans = (2 * reach + 1)[:, None, None]
    reach_cube = reach[:, None, None]
    picked = jnp.remainder(raw_bits, spans) - reach_cube
    slot_ids = jnp.arange(SLOTS, dtype=jnp.int32)[None, None, :]
    picked = jnp.where(slot_ids == 0, reach_cube, jnp.where(slot_ids == 1, -reach_cube, picked))
    return picked.astype(jnp.int32)


def shard_levels(key, shape, pieces, least, top_value):
    def one(position, blocks):
        heights = jax.random.uniform(jax.random.fold_in(jax.random.fold_in(key, 6), position), (blocks,), jnp.float32, least / len(pieces), top_value / len(pieces))
        return jnp.repeat(jnp.exp(heights), shape[position] // blocks).reshape((-1,) + (1,) * (len(shape) - position - 1))

    loudness = one(*pieces[0])
    for cut in pieces[1:]:
        loudness = loudness * one(*cut)
    return loudness


def normal_values(rng, shape, scale, bound, split=(), kind=jnp.bfloat16):
    gain = shard_levels(rng, shape, split, -0.22, 0.18) if split else 1.0
    result = jax.random.normal(rng, shape, jnp.float32) * scale * gain
    return jnp.minimum(jnp.maximum(result, -bound), bound).astype(kind)


def setup_inputs(seed: int = 0) -> dict:
    key_list = jax.random.split(jax.random.key(seed), 8)
    return {
        "state_field": normal_values(key_list[0], (NLAT, NLON, C), 1.0, 6.0, ((0, 16), (1, 32))),
        "support_offsets": draw_support_offsets(jax.random.fold_in(key_list[7], 71), 0),
        "kernel_values": normal_values(key_list[2], (K, NLAT, 2 * RAD + 1, SLOTS), ((2 * RAD + 1) * SLOTS) ** -0.5, 1.0),
        "basis_weight": normal_values(key_list[3], (K, C, C), (K * C) ** -0.5, 0.21875),
        "weight_in": normal_values(key_list[4], (C, FF), C ** -0.5, 0.375),
        "weight_out": normal_values(key_list[5], (FF, C), FF ** -0.5, 0.1875),
        "cotangent": normal_values(key_list[6], (NLAT, NLON, C), 1.0, 6.0, ((0, 16), (1, 32))),
    }


def cycle_terms(padded, support_offsets, kernel_values, cycle_id):
    window = lax.dynamic_slice_in_dim(padded, cycle_id, 2 * RAD + 1, 0)
    shifts = lax.dynamic_index_in_dim(support_offsets, cycle_id, 0, keepdims=False)
    columns = jnp.remainder(jnp.arange(NLON, dtype=jnp.int32)[None, None, :] + shifts[:, :, None], NLON)
    picked = window[jnp.arange(2 * RAD + 1, dtype=jnp.int32)[:, None, None], columns]
    weights_here = lax.dynamic_index_in_dim(kernel_values, cycle_id, 1, keepdims=False)
    return jnp.einsum('rsjc,krs->kjc', picked.astype(jnp.float32), weights_here.astype(jnp.float32))

def reference(state_field, support_offsets, kernel_values, basis_weight, weight_in, weight_out, cotangent):
    padded = jnp.pad(state_field, ((RAD, RAD), (0, 0), (0, 0)))
    grad_scale = 1.0 / math.sqrt(NLAT * NLON)
    mixing = basis_weight.astype(jnp.float32)

    def forward_cycle(carried, cycle_id):
        kernel_sum, inner_sum, outer_sum = carried
        basis_out = cycle_terms(padded, support_offsets, kernel_values, cycle_id).astype(jnp.bfloat16)
        mixed_rows = jnp.einsum('kjc,kcd->jd', basis_out.astype(jnp.float32), mixing).astype(jnp.bfloat16)
        preactivation = jnp.dot(mixed_rows, weight_in, preferred_element_type=jnp.float32)
        hidden = jax.nn.gelu(preactivation).astype(jnp.bfloat16)
        own_row = lax.dynamic_index_in_dim(state_field, cycle_id, 0, keepdims=False)
        block_row = (own_row.astype(jnp.float32) + jnp.dot(hidden, weight_out, preferred_element_type=jnp.float32)).astype(jnp.bfloat16)
        cot_row = lax.dynamic_index_in_dim(cotangent, cycle_id, 0, keepdims=False)
        outer_sum = outer_sum + jnp.dot(hidden.T, cot_row, preferred_element_type=jnp.float32)
        upstream = jnp.dot(cot_row, weight_out.T, preferred_element_type=jnp.float32)
        grad_pre = jax.vjp(jax.nn.gelu, preactivation)[1](upstream)[0].astype(jnp.bfloat16)
        inner_sum = inner_sum + jnp.dot(mixed_rows.T, grad_pre, preferred_element_type=jnp.float32)
        grad_mixed = jnp.dot(grad_pre, weight_in.T, preferred_element_type=jnp.float32).astype(jnp.bfloat16)
        kernel_sum = kernel_sum + jnp.einsum('kjc,jd->kcd', basis_out.astype(jnp.float32), grad_mixed.astype(jnp.float32))
        grad_basis = jnp.einsum('jd,kcd->kjc', grad_mixed.astype(jnp.float32), mixing).astype(jnp.bfloat16)
        return ((kernel_sum, inner_sum, outer_sum), (block_row, grad_basis))
    starting = (jnp.zeros((K, C, C), jnp.float32), jnp.zeros((C, FF), jnp.float32), jnp.zeros((FF, C), jnp.float32))
    sums, stacked = lax.scan(forward_cycle, starting, jnp.arange(NLAT, dtype=jnp.int32))
    block_out, grad_basis_all = stacked
    grad_padded = jnp.pad(grad_basis_all, ((RAD, RAD), (0, 0), (0, 0), (0, 0)))
    offsets_padded = jnp.pad(support_offsets, ((RAD, RAD), (0, 0), (0, 0)))
    values_padded = jnp.pad(kernel_values, ((0, 0), (RAD, RAD), (0, 0), (0, 0)))

    def adjoint_cycle(carried, cycle_id):
        accumulated = jnp.zeros((NLON, C), jnp.float32)
        for offset_row in range(2 * RAD + 1):
            source = cycle_id + 2 * RAD - offset_row
            grad_block = lax.dynamic_index_in_dim(grad_padded, source, 0, keepdims=False)
            shifts = lax.dynamic_index_in_dim(offsets_padded, source, 0, keepdims=False)[offset_row]
            weights_here = lax.dynamic_index_in_dim(values_padded, source, 1, keepdims=False)[:, offset_row]
            columns = jnp.remainder(jnp.arange(NLON, dtype=jnp.int32)[None, :] - shifts[:, None], NLON)
            picked = grad_block[:, columns]
            accumulated = accumulated + jnp.einsum('ksjc,ks->jc', picked.astype(jnp.float32), weights_here.astype(jnp.float32))
        cot_row = lax.dynamic_index_in_dim(cotangent, cycle_id, 0, keepdims=False)
        return (carried, (cot_row.astype(jnp.float32) + accumulated).astype(jnp.bfloat16))
    _, grad_field = lax.scan(adjoint_cycle, jnp.zeros((), jnp.float32), jnp.arange(NLAT, dtype=jnp.int32))
    kernel_sum, inner_sum, outer_sum = sums
    return (block_out, grad_field, (kernel_sum * grad_scale).astype(jnp.bfloat16), (inner_sum * grad_scale).astype(jnp.bfloat16), (outer_sum * grad_scale).astype(jnp.bfloat16))
```

```python
import math

import jax
import jax.numpy as jnp
from jax import lax
from jax.sharding import Mesh
from jax.sharding import PartitionSpec as P

RAD = 2
WIDE = 8

FINE = (("z_hi", 4), ("x", 4), ("z_mid", 2), ("z_low", 2), ("y", 4), ("core", 2))
LAT = ("z_hi", "x")
LON = ("z_mid", "z_low", "y", "core")
NEAR = ("x", "z_low", "y", "core")
FAR = ("z_hi", "z_mid")
LANES = 128


def columns_first(matrix):
    rows, cols = matrix.shape
    return [matrix[:, c : c + LANES] for c in range(0, cols, LANES)]


def total_over_devices(terms, scale):
    near, far = lax.axis_size(NEAR), lax.axis_size(FAR)
    flat = [term.reshape(-1, term.shape[-1]) for term in terms]
    blocks = [block.astype(jnp.bfloat16) for term in flat for block in columns_first(term)]
    packed = jnp.concatenate(blocks, axis=0).reshape(near, -1, LANES)
    shares = lax.all_to_all(packed, NEAR, 0, 0)
    share = jnp.sum(shares.astype(jnp.float32), axis=0).astype(jnp.bfloat16)
    spread = jnp.broadcast_to(share[None], (far,) + share.shape)
    planes = lax.all_to_all(spread, FAR, 0, 0)
    done = (jnp.sum(planes.astype(jnp.float32), axis=0) * scale).astype(jnp.bfloat16)
    copies = jnp.broadcast_to(done[None], (near,) + done.shape)
    whole = lax.all_to_all(copies, NEAR, 0, 0).reshape(-1, LANES)
    outs, start = [], 0
    for term, matrix in zip(terms, flat):
        rows, cols = matrix.shape
        pieces = []
        for _ in range(0, cols, LANES):
            pieces.append(whole[start : start + rows])
            start += rows
        outs.append(jnp.concatenate(pieces, axis=1).reshape(term.shape))
    return tuple(outs)


def with_halo(cells, sides, width, closed):
    for axis, dim in sides:
        count = lax.axis_size(axis)
        ends = count if closed else count - 1
        head = lax.slice_in_dim(cells, 0, width, axis=dim)
        tail = lax.slice_in_dim(cells, cells.shape[dim] - width, cells.shape[dim], axis=dim)
        cells = jnp.concatenate(
            [
                lax.ppermute(tail, axis, [(i, (i + 1) % count) for i in range(ends)]),
                cells,
                lax.ppermute(head, axis, [((i + 1) % count, i) for i in range(ends)]),
            ],
            axis=dim,
        )
    return cells


def banded(values, shifts, out_cols, sign):
    in_cols = out_cols + 2 * WIDE
    source_ids = jnp.arange(in_cols, dtype=jnp.int32)[None, None, :, None]
    target_ids = jnp.arange(out_cols, dtype=jnp.int32)[None, None, None, :]
    aimed = target_ids + WIDE + sign * shifts[:, :, None, None]
    onehot = (source_ids == aimed).astype(jnp.float32)
    matrix = jnp.einsum(
        "kis,ismj->kimj", values.astype(jnp.float32), onehot, precision=lax.Precision.HIGHEST
    )
    high_part = matrix.astype(jnp.bfloat16)
    low_part = (matrix - high_part.astype(jnp.float32)).astype(jnp.bfloat16)
    return (high_part, low_part)


def local(
    state_field, support_offsets, kernel_values, basis_weight, weight_in, weight_out, cotangent
):
    band_rows, band_cols, channels = state_field.shape
    lag_count = 2 * RAD + 1
    band_start = lax.axis_index(LAT) * band_rows
    local_offsets = lax.dynamic_slice_in_dim(support_offsets, band_start, band_rows, 0)
    local_values = lax.dynamic_slice_in_dim(kernel_values, band_start, band_rows, 1)
    widened = with_halo(state_field, ((LON, 1),), WIDE, True)
    extended = with_halo(widened, ((LAT, 0),), RAD, False)
    basis_sum = jnp.zeros((basis_weight.shape[0], band_rows, band_cols, channels), jnp.float32)
    for offset_row in range(lag_count):
        high_part, low_part = banded(
            local_values[:, :, offset_row, :], local_offsets[:, offset_row, :], band_cols, 1
        )
        window = extended[offset_row : offset_row + band_rows]
        basis_sum = basis_sum + jnp.einsum(
            "kimj,imc->kijc", high_part, window, preferred_element_type=jnp.float32
        )
        basis_sum = basis_sum + jnp.einsum(
            "kimj,imc->kijc", low_part, window, preferred_element_type=jnp.float32
        )
    basis_out = basis_sum.astype(jnp.bfloat16)
    mixed_grid = jnp.einsum(
        "kijc,kcd->ijd", basis_out, basis_weight, preferred_element_type=jnp.float32
    ).astype(jnp.bfloat16)
    mixed_rows = mixed_grid.reshape(-1, channels)
    preactivation = jnp.dot(mixed_rows, weight_in, preferred_element_type=jnp.float32)
    hidden = jax.nn.gelu(preactivation).astype(jnp.bfloat16)
    branch_out = jnp.dot(hidden, weight_out, preferred_element_type=jnp.float32).reshape(
        state_field.shape
    )
    block_out = (state_field.astype(jnp.float32) + branch_out).astype(jnp.bfloat16)
    cot_flat = cotangent.reshape(-1, channels)
    upstream = jnp.dot(cot_flat, weight_out.T, preferred_element_type=jnp.float32)
    grad_pre = jax.vjp(jax.nn.gelu, preactivation)[1](upstream)[0].astype(jnp.bfloat16)
    grad_mixed = jnp.dot(grad_pre, weight_in.T, preferred_element_type=jnp.float32).astype(
        jnp.bfloat16
    )
    grad_grid = grad_mixed.reshape(state_field.shape)
    kernel_term = jnp.einsum(
        "kijc,ijd->kcd", basis_out, grad_grid, preferred_element_type=jnp.float32
    )
    inner_term = jnp.dot(mixed_rows.T, grad_pre, preferred_element_type=jnp.float32)
    outer_term = jnp.dot(hidden.T, cot_flat, preferred_element_type=jnp.float32)
    grad_basis = jnp.einsum(
        "ijd,kcd->kijc", grad_grid, basis_weight, preferred_element_type=jnp.float32
    ).astype(jnp.bfloat16)
    landing = jnp.zeros((band_rows + 2 * RAD, band_cols + 2 * WIDE, channels), jnp.float32)
    for offset_row in range(lag_count):
        high_part, low_part = banded(
            local_values[:, :, offset_row, :], local_offsets[:, offset_row, :], band_cols, 1
        )
        spread = jnp.einsum(
            "kimj,kijc->imc", high_part, grad_basis, preferred_element_type=jnp.float32
        )
        spread = spread + jnp.einsum(
            "kimj,kijc->imc", low_part, grad_basis, preferred_element_type=jnp.float32
        )
        landing = landing + jnp.pad(spread, ((offset_row, 2 * RAD - offset_row), (0, 0), (0, 0)))
    rim_cells = jnp.concatenate([landing[:, :WIDE], landing[:, band_cols + WIDE :]], axis=1)
    arrived = with_halo(rim_cells.astype(jnp.bfloat16), ((LON, 1),), WIDE, True).astype(
        rim_cells.dtype
    )
    middle = landing[:, WIDE : WIDE + band_cols]
    middle = middle.at[:, :WIDE].add(arrived[:, :WIDE])
    middle = middle.at[:, band_cols - WIDE :].add(arrived[:, 3 * WIDE :])
    edge_rows = jnp.concatenate([middle[:RAD], middle[band_rows + RAD :]], axis=0)
    arrived_rows = with_halo(edge_rows.astype(jnp.bfloat16), ((LAT, 0),), RAD, False).astype(
        edge_rows.dtype
    )
    core_rows = middle[RAD : RAD + band_rows]
    core_rows = core_rows.at[:RAD].add(arrived_rows[:RAD])
    adjoint = core_rows.at[band_rows - RAD :].add(arrived_rows[3 * RAD :])
    grad_field = (cotangent.astype(jnp.float32) + adjoint).astype(jnp.bfloat16)
    grad_scale = 1.0 / math.sqrt(
        band_rows * lax.axis_size(LAT) * band_cols * lax.axis_size(LON)
    )
    finished = total_over_devices((kernel_term, inner_term, outer_term), grad_scale)
    return (block_out, grad_field, finished[0], finished[1], finished[2])


def solution(mesh):
    names, sizes = zip(*FINE)
    mesh = Mesh(mesh.devices.reshape(sizes), names)
    return jax.shard_map(
        local,
        mesh=mesh,
        in_specs=(P(LAT, LON, None), P(), P(), P(), P(), P(), P(LAT, LON, None)),
        out_specs=(P(LAT, LON, None), P(LAT, LON, None), P(), P(), P()),
        check_vma=False,
    )
```

```python
import functools
import math

import jax
import jax.numpy as jnp
from jax import lax
from jax.experimental import pallas as pl
from jax.experimental.pallas import tpu as pltpu
from jax.sharding import Mesh
from jax.sharding import PartitionSpec as P

RAD = 2
WIDE = 8
LAGS = 2 * RAD + 1

FINE = (("z_hi", 4), ("x", 4), ("z_mid", 2), ("z_low", 2), ("y", 4), ("core", 2))
LAT = ("z_hi", "x")
LON = ("z_mid", "z_low", "y", "core")
NEAR = ("x", "z_low", "y", "core")
FAR = ("z_hi", "z_mid")
LANES = 128
CHUNK = 256

ROWS, COLS = ((0,), (0,)), ((1,), (1,))
VMEM = pl.BlockSpec(memory_space=pltpu.VMEM)
SMEM = pl.BlockSpec(memory_space=pltpu.SMEM)


def dot(a, b, contract=((1,), (0,))):
    return lax.dot_general(a, b, (contract, ((), ())), preferred_element_type=jnp.float32)


def kernel_call(body, operands, specs, outs, scratch=(), flops=0, mib=24, name=None):
    moved = sum(x.size * x.dtype.itemsize for x in (*operands, *outs))
    return pl.pallas_call(
        body,
        out_shape=tuple(outs),
        in_specs=specs,
        out_specs=tuple(VMEM for _ in outs),
        scratch_shapes=scratch,
        compiler_params=pltpu.CompilerParams(vmem_limit_bytes=mib << 20),
        cost_estimate=pl.CostEstimate(flops=flops, bytes_accessed=moved, transcendentals=0),
        name=name,
    )(*operands)


def like(shape, dtype):
    return jax.ShapeDtypeStruct(shape, dtype)


def prepare_kernel(cols, offset_ref, value_ref, cot_ref, out_ref, high_ref, low_ref, up_ref):
    up_ref[...] = dot(cot_ref[...], out_ref[...], COLS)
    kinds, cycles, lags, slots = 3, high_ref.shape[0] // (3 * cols), LAGS, offset_ref.shape[0]
    slots = slots // (cycles * lags)
    span = cols + 2 * WIDE
    shape = (cols, LANES)
    ahead = lax.broadcasted_iota(jnp.int32, shape, 1) - lax.broadcasted_iota(jnp.int32, shape, 0)

    def cycle(i, carry):
        for start in range(0, high_ref.shape[1], LANES):
            sums = [jnp.zeros(shape, jnp.float32) for _ in range(kinds)]
            for q in range(lags):
                if q * span >= start + LANES or (q + 1) * span <= start:
                    continue
                for s in range(slots):
                    at = (i * lags + q) * slots + s
                    hit = ahead == offset_ref[at] + (q * span + WIDE - start)
                    for k in range(kinds):
                        value = value_ref[k * cycles * lags * slots + at]
                        sums[k] = sums[k] + jnp.where(hit, value, 0.0)
            for k in range(kinds):
                at = pl.ds(pl.multiple_of((i * kinds + k) * cols, cols), cols)
                high = sums[k].astype(jnp.bfloat16)
                high_ref[at, start : start + LANES] = high
                rest = sums[k] - high.astype(jnp.float32)
                low_ref[at, start : start + LANES] = rest.astype(jnp.bfloat16)
        return carry

    lax.fori_loop(0, cycles, cycle, 0)


def gelu_and_slope(x):
    c, a = math.sqrt(2.0 / math.pi), 0.044715
    square = x * x
    t = jnp.tanh(c * (x + a * (square * x)))
    cdf = 0.5 * (1.0 + t)
    slope = cdf + (0.5 * x) * (1.0 - t * t) * (c * (1.0 + (3.0 * a) * square))
    return x * cdf, slope


def main_kernel(
    high_ref, low_ref, top_ref, state_ref, bottom_ref, left_ref, right_ref, cot_ref, up_ref, mix_ref, in_ref,
    packed_ref, hidden_ref, grad_ref, cells_ref, basis_ref,
):
    rows, cols, channels = state_ref.shape
    span = cols + 2 * WIDE
    kinds = basis_ref.shape[0]
    for r in range(rows + 2 * RAD):
        if r < RAD:
            middle = top_ref[r]
        elif r < RAD + rows:
            middle = state_ref[r - RAD]
        else:
            middle = bottom_ref[r - RAD - rows]
        parts = [left_ref[r], middle, right_ref[r]]
        line = jnp.concatenate([part.astype(jnp.float32) for part in parts], axis=0)
        cells_ref[r * span : (r + 1) * span] = line.astype(jnp.bfloat16)
    used = (rows + 2 * RAD) * span
    cells_ref[used:] = jnp.zeros((cells_ref.shape[0] - used, channels), jnp.bfloat16)

    depth = high_ref.shape[1]
    for i in range(rows):
        window = cells_ref[i * span : i * span + depth]
        at = slice(i * kinds * cols, (i + 1) * kinds * cols)
        taken = dot(high_ref[at], window) + dot(low_ref[at], window)
        for k in range(kinds):
            piece = taken[k * cols : (k + 1) * cols].astype(jnp.bfloat16)
            basis_ref[k, i * cols : (i + 1) * cols] = piece
    mixed = sum(dot(basis_ref[k], mix_ref[k]) for k in range(kinds)).astype(jnp.bfloat16)

    cot = cot_ref[...]
    start = 0

    def pack(matrix, place, height):
        for c in range(0, matrix.shape[1], LANES):
            at = place + (c // LANES) * height
            packed_ref[at : at + matrix.shape[0]] = matrix[:, c : c + LANES].astype(jnp.bfloat16)

    units = in_ref.shape[1]
    outer_at, inner_at = 0, units * (channels // LANES)
    basis_at = inner_at + channels * (units // LANES)
    back = jnp.zeros((rows * cols, channels), jnp.float32)
    for c in range(0, units, CHUNK):
        weight = in_ref[:, c : c + CHUNK]
        hidden, slope = gelu_and_slope(dot(mixed, weight))
        hidden = hidden.astype(jnp.bfloat16)
        grad_pre = (up_ref[:, c : c + CHUNK] * slope).astype(jnp.bfloat16)
        hidden_ref[:, c : c + CHUNK] = hidden
        back = back + dot(grad_pre, weight, COLS)
        pack(dot(hidden, cot, ROWS), outer_at + c, units)
        pack(dot(mixed, grad_pre, ROWS), inner_at + (c // LANES) * channels, channels)
    grad_mixed = back.astype(jnp.bfloat16)
    grad_ref[...] = grad_mixed
    for k in range(kinds):
        pack(dot(basis_ref[k], grad_mixed, ROWS), basis_at + k * channels, kinds * channels)


def adjoint_kernel(
    grad_ref, mix_ref, high_ref, low_ref, hidden_ref, out_ref, state_ref,
    left_ref, right_ref, middle_ref, block_ref, back_ref, landing_ref,
):
    rows, cols, channels = state_ref.shape
    span = cols + 2 * WIDE
    kinds = mix_ref.shape[0]
    grad = grad_ref[...]
    for k in range(kinds):
        back_ref[k] = dot(grad, mix_ref[k], COLS).astype(jnp.bfloat16)
    landing_ref[...] = jnp.zeros_like(landing_ref)
    depth = high_ref.shape[1]
    for i in range(rows):
        pieces = [back_ref[k, i * cols : (i + 1) * cols] for k in range(kinds)]
        taken = jnp.concatenate(pieces, axis=0)
        at = slice(i * kinds * cols, (i + 1) * kinds * cols)
        spread = dot(high_ref[at], taken, ROWS) + dot(low_ref[at], taken, ROWS)
        landing_ref[i * span : i * span + depth] += spread
    for r in range(rows + 2 * RAD):
        line = landing_ref[r * span : (r + 1) * span]
        left_ref[r] = line[:WIDE].astype(jnp.bfloat16)
        middle_ref[r] = line[WIDE : WIDE + cols]
        right_ref[r] = line[WIDE + cols :].astype(jnp.bfloat16)
    branch = dot(hidden_ref[...], out_ref[...])
    for i in range(rows):
        line = state_ref[i].astype(jnp.float32) + branch[i * cols : (i + 1) * cols]
        block_ref[i] = line.astype(jnp.bfloat16)


def rims_kernel(middle_ref, left_ref, right_ref, top_ref, bottom_ref, core_ref):
    rows, cols = core_ref.shape[:2]
    for r in range(rows + 2 * RAD):
        line = middle_ref[r]
        head = line[:WIDE] + left_ref[r].astype(jnp.float32)
        tail = line[cols - WIDE :] + right_ref[r].astype(jnp.float32)
        line = jnp.concatenate([head, line[WIDE : cols - WIDE], tail], axis=0)
        if r < RAD:
            top_ref[r] = line.astype(jnp.bfloat16)
        elif r < RAD + rows:
            core_ref[r - RAD] = line
        else:
            bottom_ref[r - RAD - rows] = line.astype(jnp.bfloat16)


def field_kernel(cot_ref, core_ref, above_ref, below_ref, field_ref):
    rows = core_ref.shape[0]
    for r in range(rows):
        line = core_ref[r]
        if r < RAD:
            line = line + above_ref[r].astype(jnp.float32)
        if r >= rows - RAD:
            line = line + below_ref[r - rows + RAD].astype(jnp.float32)
        field_ref[r] = (cot_ref[r].astype(jnp.float32) + line).astype(jnp.bfloat16)


def sum_kernel(scale, parts_ref, *refs):
    out_ref = refs[-1]
    total = parts_ref[0].astype(jnp.float32)
    for i in range(1, parts_ref.shape[0]):
        total = total + parts_ref[i].astype(jnp.float32)
    total = (total * scale).astype(out_ref.dtype)
    for i in range(out_ref.shape[0]):
        out_ref[i] = total


def sum_and_copy(parts, scale, copies, *later_than):
    return kernel_call(
        functools.partial(sum_kernel, scale),
        (parts, *later_than),
        [VMEM] + [pl.BlockSpec(memory_space=pl.ANY)] * len(later_than),
        [like((copies,) + parts.shape[1:], jnp.bfloat16)],
        flops=parts.size,
        mib=16,
        name="sum_and_copy",
    )[0]


def unpack(whole, shapes):
    flat, outs, start = whole.reshape(-1, LANES), [], 0
    for rows, cols in shapes:
        pieces = []
        for _ in range(0, cols, LANES):
            pieces.append(flat[start : start + rows])
            start += rows
        outs.append(jnp.concatenate(pieces, axis=1))
    return outs


def shift(cells, axes, step, closed):
    count = lax.axis_size(axes)
    pairs = [(i, (i + step) % count) for i in range(count) if closed or 0 <= i + step < count]
    return lax.ppermute(cells, axes, pairs)


def local(
    state_field, support_offsets, kernel_values, basis_weight, weight_in, weight_out, cotangent
):
    rows, cols, channels = state_field.shape
    kinds, units = basis_weight.shape[0], weight_in.shape[1]
    cells, span = rows * cols, cols + 2 * WIDE
    tall = rows + 2 * RAD
    depth = -(-LAGS * span // LANES) * LANES
    near, far = lax.axis_size(NEAR), lax.axis_size(FAR)
    cot_flat = cotangent.reshape(cells, channels)
    f32, bf16 = jnp.float32, jnp.bfloat16

    top = shift(state_field[rows - RAD :], LAT, 1, False)
    bottom = shift(state_field[:RAD], LAT, -1, False)
    heads = jnp.concatenate([top[:, :WIDE], state_field[:, :WIDE], bottom[:, :WIDE]], axis=0)
    tails = jnp.concatenate(
        [top[:, cols - WIDE :], state_field[:, cols - WIDE :], bottom[:, cols - WIDE :]], axis=0
    )
    left = shift(tails, LON, 1, True)
    right = shift(heads, LON, -1, True)

    band_start = lax.axis_index(LAT) * rows
    offsets = lax.dynamic_slice_in_dim(support_offsets, band_start, rows, 0)
    values = lax.dynamic_slice_in_dim(kernel_values, band_start, rows, 1).astype(f32)
    band_shape = (rows * kinds * cols, depth)
    high, low, upstream = kernel_call(
        functools.partial(prepare_kernel, cols),
        (offsets.reshape(-1), values.reshape(-1), cot_flat, weight_out),
        [SMEM, SMEM, VMEM, VMEM],
        [like(band_shape, bf16), like(band_shape, bf16), like((cells, units), f32)],
        flops=8 * cells * channels * units,
        name="prepare",
    )
    packed_rows = channels * (2 * units + kinds * channels) // LANES
    packed, hidden, grad_mixed = kernel_call(
        main_kernel,
        (high, low, top, state_field, bottom, left, right, cot_flat, upstream, basis_weight, weight_in),
        [VMEM] * 11,
        [like((packed_rows, LANES), bf16), like((cells, units), bf16), like((cells, channels), bf16)],
        [
            pltpu.VMEM((rows * span + depth, channels), bf16),
            pltpu.VMEM((kinds, cells, channels), bf16),
        ],
        flops=8 * cells * channels * units,
        mib=32,
        name="main",
    )

    shares = lax.all_to_all(packed.reshape(near, -1, LANES), NEAR, 0, 0)

    to_left, to_right, middle, block_out = kernel_call(
        adjoint_kernel,
        (grad_mixed, basis_weight, high, low, hidden, weight_out, state_field),
        [VMEM] * 7,
        [
            like((tall, WIDE, channels), bf16),
            like((tall, WIDE, channels), bf16),
            like((tall, cols, channels), f32),
            like(state_field.shape, bf16),
        ],
        [
            pltpu.VMEM((kinds, cells, channels), bf16),
            pltpu.VMEM((rows * span + depth, channels), f32),
        ],
        flops=4 * cells * channels * units,
        mib=32,
        name="adjoint",
    )
    from_left = shift(to_right, LON, 1, True)
    from_right = shift(to_left, LON, -1, True)
    planes = sum_and_copy(shares, 1.0, far, from_left, from_right)
    planes = lax.all_to_all(planes, FAR, 0, 0)
    rim = like((RAD, cols, channels), bf16)
    to_above, to_below, core = kernel_call(
        rims_kernel,
        (middle, from_left, from_right),
        [VMEM] * 3,
        [rim, rim, like(state_field.shape, f32)],
        name="rims",
    )
    above = shift(to_below, LAT, 1, False)
    below = shift(to_above, LAT, -1, False)
    scale = 1.0 / math.sqrt(cells * lax.axis_size(LAT) * lax.axis_size(LON))
    copies = sum_and_copy(planes, scale, near, core)
    whole = lax.all_to_all(copies, NEAR, 0, 0)
    (grad_field,) = kernel_call(
        field_kernel,
        (cotangent, core, above, below),
        [VMEM] * 4,
        [like(state_field.shape, bf16)],
        name="field",
    )
    shapes = ((units, channels), (channels, units), (kinds * channels, channels))
    grad_out, grad_in, grad_basis = unpack(whole, shapes)
    return (block_out, grad_field, grad_basis.reshape(basis_weight.shape), grad_in, grad_out)


def solution(mesh):
    names, sizes = zip(*FINE)
    mesh = Mesh(mesh.devices.reshape(sizes), names)
    return jax.shard_map(
        local,
        mesh=mesh,
        in_specs=(P(LAT, LON, None), P(), P(), P(), P(), P(), P(LAT, LON, None)),
        out_specs=(P(LAT, LON, None), P(LAT, LON, None), P(), P(), P()),
        check_vma=False,
    )
```

```python
import functools
import math

import jax
import jax.numpy as jnp
from jax import lax
from jax.experimental import pallas as pl
from jax.experimental.pallas import tpu as pltpu
from jax.sharding import Mesh
from jax.sharding import PartitionSpec as P

RAD = 2
WIDE = 8
LAGS = 2 * RAD + 1

FINE = (("z_hi", 4), ("x", 4), ("z_mid", 2), ("z_low", 2), ("y", 4), ("core", 2))
LAT = ("z_hi", "x")
LON = ("z_mid", "z_low", "y", "core")
CORE = "core"
NEAR = ("x", "z_low", "y")
FAR = ("z_hi", "z_mid")
LANES = 128
CHUNK = 256

ROWS, COLS = ((0,), (0,)), ((1,), (1,))
VMEM = pl.BlockSpec(memory_space=pltpu.VMEM)
SMEM = pl.BlockSpec(memory_space=pltpu.SMEM)
ANY = pl.BlockSpec(memory_space=pl.ANY)


def dot(a, b, contract=((1,), (0,))):
    return lax.dot_general(a, b, (contract, ((), ())), preferred_element_type=jnp.float32)


def kernel_call(body, operands, specs, outs, scratch=(), flops=0, mib=16, name=None):
    moved = sum(x.size * x.dtype.itemsize for x in (*operands, *outs))
    return pl.pallas_call(
        body,
        out_shape=tuple(outs),
        in_specs=specs,
        out_specs=tuple(VMEM for _ in outs),
        scratch_shapes=scratch,
        compiler_params=pltpu.CompilerParams(vmem_limit_bytes=mib << 20),
        cost_estimate=pl.CostEstimate(flops=flops, bytes_accessed=moved, transcendentals=0),
        name=name,
    )(*operands)


def like(shape, dtype):
    return jax.ShapeDtypeStruct(shape, dtype)


def bands_kernel(cols, offset_ref, value_ref, high_ref, low_ref):
    kinds, cycles, lags, slots = 3, high_ref.shape[0] // (3 * cols), LAGS, offset_ref.shape[0]
    slots = slots // (cycles * lags)
    span = cols + 2 * WIDE
    shape = (cols, LANES)
    ahead = lax.broadcasted_iota(jnp.int32, shape, 1) - lax.broadcasted_iota(jnp.int32, shape, 0)

    def cycle(i, carry):
        for start in range(0, high_ref.shape[1], LANES):
            sums = [jnp.zeros(shape, jnp.float32) for _ in range(kinds)]
            for q in range(lags):
                if q * span >= start + LANES or (q + 1) * span <= start:
                    continue
                for s in range(slots):
                    at = (i * lags + q) * slots + s
                    hit = ahead == offset_ref[at] + (q * span + WIDE - start)
                    for k in range(kinds):
                        value = value_ref[k * cycles * lags * slots + at]
                        sums[k] = sums[k] + jnp.where(hit, value, 0.0)
            for k in range(kinds):
                at = pl.ds(pl.multiple_of((i * kinds + k) * cols, cols), cols)
                high = sums[k].astype(jnp.bfloat16)
                high_ref[at, start : start + LANES] = high
                rest = sums[k] - high.astype(jnp.float32)
                low_ref[at, start : start + LANES] = rest.astype(jnp.bfloat16)
        return carry

    lax.fori_loop(0, cycles, cycle, 0)


def by_side(odd, near, far):
    near, far = near.astype(jnp.float32), far.astype(jnp.float32)
    return jnp.where(odd, near, far), jnp.where(odd, far, near)


def by_partner(odd, before, after):
    near, far = jnp.where(odd, before, after), jnp.where(odd, after, before)
    return near.astype(jnp.bfloat16), far.astype(jnp.bfloat16)


def whole_rows(side_ref, near_ref, state_ref, far_ref):
    above, below = [], []
    for r in range(RAD):
        first, second = by_side(side_ref[0] != 0, near_ref[r], far_ref[r])
        above.append(first)
        below.append(second)
    return above + [state_ref[r].astype(jnp.float32) for r in range(state_ref.shape[0])] + below


def gelu_and_slope(x):
    c, a = math.sqrt(2.0 / math.pi), 0.044715
    square = x * x
    t = jnp.tanh(c * (x + a * (square * x)))
    cdf = 0.5 * (1.0 + t)
    slope = cdf + (0.5 * x) * (1.0 - t * t) * (c * (1.0 + (3.0 * a) * square))
    return x * cdf, slope


def fetch(sources, targets, sems):
    copies = [
        pltpu.make_async_copy(source, target, sems.at[i])
        for i, (source, target) in enumerate(zip(sources, targets))
    ]
    for copy in copies:
        copy.start()

    def take(i):
        copies[i].wait()
        return targets[i]

    return take


def main_kernel(
    side_ref, high_ref, low_ref, lat_near_ref, state_ref, lat_far_ref, lon_near_ref, lon_far_ref,
    mix_hbm, in_hbm, out_hbm, cot_hbm, packed_ref, hidden_ref, grad_ref,
    cells_ref, basis_ref, mix_ref, in_ref, out_ref, cot_ref, sems,
):
    take = fetch((mix_hbm, in_hbm, out_hbm, cot_hbm), (mix_ref, in_ref, out_ref, cot_ref), sems)
    rows, cols, channels = state_ref.shape
    span = cols + 2 * WIDE
    kinds = basis_ref.shape[0]
    for r, line in enumerate(whole_rows(side_ref, lat_near_ref, state_ref, lat_far_ref)):
        left, right = by_side(side_ref[1] != 0, lon_near_ref[r], lon_far_ref[r])
        line = jnp.concatenate([left, line, right], axis=0)
        cells_ref[r * span : (r + 1) * span] = line.astype(jnp.bfloat16)
    used = (rows + 2 * RAD) * span
    cells_ref[used:] = jnp.zeros((cells_ref.shape[0] - used, channels), jnp.bfloat16)

    depth = high_ref.shape[1]
    for i in range(rows):
        window = cells_ref[i * span : i * span + depth]
        at = slice(i * kinds * cols, (i + 1) * kinds * cols)
        taken = dot(high_ref[at], window) + dot(low_ref[at], window)
        for k in range(kinds):
            piece = taken[k * cols : (k + 1) * cols].astype(jnp.bfloat16)
            basis_ref[k, i * cols : (i + 1) * cols] = piece
    mix_ref = take(0)
    mixed = sum(dot(basis_ref[k], mix_ref[k]) for k in range(kinds)).astype(jnp.bfloat16)

    in_ref, out_ref = take(1), take(2)
    cot = take(3)[...]
    core, half = side_ref[1], packed_ref.shape[1]

    def pack(matrix, place, height):
        for c in range(0, matrix.shape[1], LANES):
            owner, at = divmod(place + (c // LANES) * height, half)
            slot = core if owner == 0 else 1 - core
            packed_ref[slot, at : at + matrix.shape[0]] = matrix[:, c : c + LANES].astype(jnp.bfloat16)

    units = in_ref.shape[1]
    outer_at, inner_at = 0, units * (channels // LANES)
    basis_at = inner_at + channels * (units // LANES)
    back = jnp.zeros((rows * cols, channels), jnp.float32)
    for c in range(0, units, CHUNK):
        weight = in_ref[:, c : c + CHUNK]
        hidden, slope = gelu_and_slope(dot(mixed, weight))
        hidden = hidden.astype(jnp.bfloat16)
        upstream = dot(cot, out_ref[c : c + CHUNK], COLS)
        grad_pre = (upstream * slope).astype(jnp.bfloat16)
        hidden_ref[:, c : c + CHUNK] = hidden
        back = back + dot(grad_pre, weight, COLS)
        pack(dot(hidden, cot, ROWS), outer_at + c, units)
        pack(dot(mixed, grad_pre, ROWS), inner_at + (c // LANES) * channels, channels)
    grad_mixed = back.astype(jnp.bfloat16)
    grad_ref[...] = grad_mixed
    for k in range(kinds):
        pack(dot(basis_ref[k], grad_mixed, ROWS), basis_at + k * channels, kinds * channels)


def adjoint_kernel(
    side_ref, grad_ref, mix_ref, high_ref, low_ref, near_ref, far_ref, middle_ref, back_ref, landing_ref
):
    tall, cols, channels = middle_ref.shape
    rows, span = tall - 2 * RAD, cols + 2 * WIDE
    kinds = mix_ref.shape[0]
    grad = grad_ref[...]
    for k in range(kinds):
        back_ref[k] = dot(grad, mix_ref[k], COLS).astype(jnp.bfloat16)
    landing_ref[...] = jnp.zeros_like(landing_ref)
    depth = high_ref.shape[1]
    for i in range(rows):
        pieces = [back_ref[k, i * cols : (i + 1) * cols] for k in range(kinds)]
        taken = jnp.concatenate(pieces, axis=0)
        at = slice(i * kinds * cols, (i + 1) * kinds * cols)
        spread = dot(high_ref[at], taken, ROWS) + dot(low_ref[at], taken, ROWS)
        landing_ref[i * span : i * span + depth] += spread
    for r in range(rows + 2 * RAD):
        line = landing_ref[r * span : (r + 1) * span]
        near_ref[r], far_ref[r] = by_partner(side_ref[1] != 0, line[:WIDE], line[WIDE + cols :])
        middle_ref[r] = line[WIDE : WIDE + cols]


def rims_kernel(side_ref, middle_ref, near_ref, far_ref, to_near_ref, to_far_ref, core_ref):
    rows, cols = core_ref.shape[:2]
    lines = []
    for r in range(rows + 2 * RAD):
        left, right = by_side(side_ref[1] != 0, near_ref[r], far_ref[r])
        line = middle_ref[r]
        head, tail = line[:WIDE] + left, line[cols - WIDE :] + right
        lines.append(jnp.concatenate([head, line[WIDE : cols - WIDE], tail], axis=0))
    for r in range(RAD):
        above, below = lines[r], lines[rows + RAD + r]
        to_near_ref[r], to_far_ref[r] = by_partner(side_ref[0] != 0, above, below)
    for r in range(rows):
        core_ref[r] = lines[RAD + r]


def field_kernel(side_ref, cot_ref, core_ref, near_ref, far_ref, field_ref):
    rows = core_ref.shape[0]
    lines = [core_ref[r] for r in range(rows)]
    for r in range(RAD):
        above, below = by_side(side_ref[0] != 0, near_ref[r], far_ref[r])
        lines[r] = lines[r] + above
        lines[rows - RAD + r] = lines[rows - RAD + r] + below
    for r in range(rows):
        field_ref[r] = (cot_ref[r].astype(jnp.float32) + lines[r]).astype(jnp.bfloat16)


def edges_kernel(side_ref, lat_near_ref, state_ref, lat_far_ref, near_ref, far_ref):
    cols = state_ref.shape[1]
    for r, line in enumerate(whole_rows(side_ref, lat_near_ref, state_ref, lat_far_ref)):
        near_ref[r], far_ref[r] = by_partner(side_ref[1] != 0, line[:WIDE], line[cols - WIDE :])


def add_kernel(a_ref, b_ref, sum_ref):
    sum_ref[...] = (a_ref[0].astype(jnp.float32) + b_ref[...].astype(jnp.float32)).astype(jnp.bfloat16)


def tie_kernel(value_ref, *refs):
    refs[-1][...] = value_ref[...]


def tie(value, *later_than):
    return kernel_call(
        tie_kernel,
        (value, *later_than),
        [VMEM] + [ANY] * len(later_than),
        [like(value.shape, value.dtype)],
        name="tie",
    )[0]


def sum_kernel(scale, parts_ref, *refs):
    out_ref = refs[-1]
    total = parts_ref[0].astype(jnp.float32)
    for i in range(1, parts_ref.shape[0]):
        total = total + parts_ref[i].astype(jnp.float32)
    total = (total * scale).astype(out_ref.dtype)
    for i in range(out_ref.shape[0]):
        out_ref[i] = total


def sum_and_copy(parts, scale, copies, *later_than):
    return kernel_call(
        functools.partial(sum_kernel, scale),
        (parts, *later_than),
        [VMEM] + [ANY] * len(later_than),
        [like((copies,) + parts.shape[1:], jnp.bfloat16)],
        flops=parts.size,
        mib=16,
        name="sum_and_copy",
    )[0]


def unpack(whole, shapes):
    outs, start = [], 0
    for rows, cols in shapes:
        pieces = []
        for _ in range(0, cols, LANES):
            pieces.append(whole[start : start + rows])
            start += rows
        outs.append(jnp.concatenate(pieces, axis=1))
    return outs


def block_kernel(hidden_ref, out_ref, state_ref, block_ref):
    rows, cols = state_ref.shape[:2]
    branch = dot(hidden_ref[...], out_ref[...])
    for i in range(rows):
        line = state_ref[i].astype(jnp.float32) + branch[i * cols : (i + 1) * cols]
        block_ref[i] = line.astype(jnp.bfloat16)


def swap(cells, axes, lead, closed):
    count = lax.axis_size(axes)
    pairs = []
    for i in range(lead, count, 2):
        if closed or i + 1 < count:
            pairs += [(i, (i + 1) % count), ((i + 1) % count, i)]
    return lax.ppermute(cells, axes, pairs)


def swap_both(near, far, axes, closed):
    far = swap(far, axes, 1, closed)
    return swap(near, axes, 0, closed), far


def local(
    state_field, support_offsets, kernel_values, basis_weight, weight_in, weight_out, cotangent
):
    rows, cols, channels = state_field.shape
    kinds, units = basis_weight.shape[0], weight_in.shape[1]
    cells, span = rows * cols, cols + 2 * WIDE
    tall = rows + 2 * RAD
    depth = -(-LAGS * span // LANES) * LANES
    near, far = lax.axis_size(NEAR), lax.axis_size(FAR)
    cot_flat = cotangent.reshape(cells, channels)
    f32, bf16 = jnp.float32, jnp.bfloat16

    odd_lat, odd_lon = lax.axis_index(LAT) % 2, lax.axis_index(LON) % 2
    sides = jnp.stack([odd_lat, odd_lon])
    last = rows - RAD
    to_near = lax.dynamic_slice_in_dim(state_field, jnp.where(odd_lat == 0, last, 0), RAD, 0)
    to_far = lax.dynamic_slice_in_dim(state_field, jnp.where(odd_lat == 0, 0, last), RAD, 0)
    lat_near, lat_far = swap_both(to_near, to_far, LAT, False)

    band_start = lax.axis_index(LAT) * rows
    offsets = lax.dynamic_slice_in_dim(support_offsets, band_start, rows, 0)
    values = lax.dynamic_slice_in_dim(kernel_values, band_start, rows, 1).astype(f32)
    band_shape = (rows * kinds * cols, depth)
    high, low = kernel_call(
        functools.partial(bands_kernel, cols),
        (offsets.reshape(-1), values.reshape(-1)),
        [SMEM, SMEM],
        [like(band_shape, bf16), like(band_shape, bf16)],
        flops=8 * cells * channels * units,
        name="bands",
    )
    rim = like((tall, WIDE, channels), bf16)
    to_near, to_far = kernel_call(
        edges_kernel,
        (sides, lat_near, state_field, lat_far),
        [SMEM] + [VMEM] * 3,
        [rim, rim],
        name="edges",
    )
    lon_near, lon_far = swap_both(to_near, to_far, LON, True)
    packed_rows = channels * (2 * units + kinds * channels) // LANES
    core = lax.axis_index(CORE)
    half = like((packed_rows // 2, LANES), bf16)
    packed, hidden, grad_mixed = kernel_call(
        main_kernel,
        (
            sides, high, low, lat_near, state_field, lat_far, lon_near, lon_far,
            basis_weight, weight_in, weight_out, cot_flat,
        ),
        [SMEM] + [VMEM] * 7 + [ANY] * 4,
        [like((2,) + half.shape, bf16), like((cells, units), bf16), like((cells, channels), bf16)],
        [
            pltpu.VMEM((rows * span + depth, channels), bf16),
            pltpu.VMEM((kinds, cells, channels), bf16),
            pltpu.VMEM(basis_weight.shape, bf16),
            pltpu.VMEM(weight_in.shape, bf16),
            pltpu.VMEM(weight_out.shape, bf16),
            pltpu.VMEM(cot_flat.shape, bf16),
            pltpu.SemaphoreType.DMA((4,)),
        ],
        flops=10 * cells * channels * units,
        name="main",
    )

    arrived = swap(packed[1], CORE, 0, True)
    chip = kernel_call(add_kernel, (packed, arrived), [VMEM] * 2, [half], name="add")[0]
    shares = lax.all_to_all(chip.reshape(near, -1, LANES), NEAR, 0, 0)

    to_near, to_far, middle = kernel_call(
        adjoint_kernel,
        (sides, grad_mixed, basis_weight, high, low),
        [SMEM] + [VMEM] * 4,
        [rim, rim, like((tall, cols, channels), f32)],
        [
            pltpu.VMEM((kinds, cells, channels), bf16),
            pltpu.VMEM((rows * span + depth, channels), f32),
        ],
        flops=4 * cells * channels * units,
        name="adjoint",
    )
    near_rim, far_rim = swap_both(to_near, to_far, LON, True)
    planes = sum_and_copy(shares, 1.0, far, near_rim, far_rim)
    planes = lax.all_to_all(planes, FAR, 0, 0)
    edge = like((RAD, cols, channels), bf16)
    to_near, to_far, inside = kernel_call(
        rims_kernel,
        (sides, middle, near_rim, far_rim),
        [SMEM] + [VMEM] * 3,
        [edge, edge, like(state_field.shape, f32)],
        name="rims",
    )
    near_edge, far_edge = swap_both(to_near, to_far, LAT, False)
    scale = 1.0 / math.sqrt(cells * lax.axis_size(LAT) * lax.axis_size(LON))
    copies = sum_and_copy(planes, scale, near, inside)
    (grad_field,) = kernel_call(
        field_kernel,
        (sides, cotangent, inside, near_edge, far_edge),
        [SMEM] + [VMEM] * 4,
        [like(state_field.shape, bf16)],
        name="field",
    )
    (block_out,) = kernel_call(
        block_kernel,
        (hidden, weight_out, state_field),
        [VMEM] * 3,
        [like(state_field.shape, bf16)],
        flops=2 * cells * channels * units,
        name="block",
    )
    mine = lax.all_to_all(copies, NEAR, 0, 0).reshape(-1, LANES)
    mine = tie(mine, near_edge, far_edge, block_out)
    other = swap(mine, CORE, 0, True)
    shapes = ((units, channels), (channels, units), (kinds * channels, channels))
    whole = jnp.concatenate(
        [jnp.where(core == 0, mine, other), jnp.where(core == 0, other, mine)], axis=0
    )
    grad_out, grad_in, grad_basis = unpack(whole, shapes)
    return (block_out, grad_field, grad_basis.reshape(basis_weight.shape), grad_in, grad_out)


def solution(mesh):
    names, sizes = zip(*FINE)
    mesh = Mesh(mesh.devices.reshape(sizes), names)
    return jax.shard_map(
        local,
        mesh=mesh,
        in_specs=(P(LAT, LON, None), P(), P(), P(), P(), P(), P(LAT, LON, None)),
        out_specs=(P(LAT, LON, None), P(LAT, LON, None), P(), P(), P()),
        check_vma=False,
    )
```

```python
import functools
import math

import jax
import jax.numpy as jnp
from jax import lax
from jax.experimental import pallas as pl
from jax.experimental.pallas import tpu as pltpu
from jax.sharding import Mesh
from jax.sharding import PartitionSpec as P

RAD = 2
WIDE = 8
LAGS = 2 * RAD + 1

FINE = (("z_hi", 4), ("x", 4), ("z_mid", 2), ("z_low", 2), ("y", 4), ("core", 2))
LAT = ("z_hi", "x")
LON = ("z_mid", "z_low", "y", "core")
CORE = "core"
NEAR = ("x", "z_low", "y")
FAR = ("z_hi", "z_mid")
LANES = 128
CHUNK = 256

ROWS, COLS = ((0,), (0,)), ((1,), (1,))
VMEM = pl.BlockSpec(memory_space=pltpu.VMEM)
SMEM = pl.BlockSpec(memory_space=pltpu.SMEM)
ANY = pl.BlockSpec(memory_space=pl.ANY)


def dot(a, b, contract=((1,), (0,))):
    return lax.dot_general(a, b, (contract, ((), ())), preferred_element_type=jnp.float32)


def kernel_call(body, operands, specs, outs, scratch=(), flops=0, mib=16, name=None):
    moved = sum(x.size * x.dtype.itemsize for x in (*operands, *outs))
    return pl.pallas_call(
        body,
        out_shape=tuple(outs),
        in_specs=specs,
        out_specs=tuple(VMEM for _ in outs),
        scratch_shapes=scratch,
        compiler_params=pltpu.CompilerParams(vmem_limit_bytes=mib << 20),
        cost_estimate=pl.CostEstimate(flops=flops, bytes_accessed=moved, transcendentals=0),
        name=name,
    )(*operands)


def like(shape, dtype):
    return jax.ShapeDtypeStruct(shape, dtype)


def bands_kernel(cols, offset_ref, value_ref, bands_ref, first_ref):
    cycles, height, depth = bands_ref.shape
    kinds, span = height // (2 * cols), cols + 2 * WIDE
    slots = offset_ref.shape[1] // LAGS
    lane = lax.broadcasted_iota(jnp.int32, (cycles, LANES), 1)
    for start in range(0, depth, LANES):
        sums = [jnp.zeros((cycles, LANES), jnp.float32) for _ in range(kinds)]
        for q in range(LAGS):
            if q * span + 2 * WIDE < start or q * span >= start + LANES:
                continue
            for s in range(slots):
                at = slice(q * slots + s, q * slots + s + 1)
                hit = lane == offset_ref[:, at] + (q * span + WIDE - start)
                for k in range(kinds):
                    sums[k] = sums[k] + jnp.where(hit, value_ref[k, :, at], 0.0)
        for k in range(kinds):
            first_ref[k, :, start : start + LANES] = sums[k]
    for i in range(cycles):
        for k in range(kinds):
            block = jnp.broadcast_to(first_ref[k, i : i + 1, :], (cols, depth))
            block = pltpu.roll(block, 0, 1, stride=1, stride_axis=0)
            high = block.astype(jnp.bfloat16)
            low = (block - high.astype(jnp.float32)).astype(jnp.bfloat16)
            bands_ref[i, k * cols : (k + 1) * cols] = high
            bands_ref[i, (kinds + k) * cols : (kinds + k + 1) * cols] = low


def by_side(odd, near, far):
    near, far = near.astype(jnp.float32), far.astype(jnp.float32)
    return jnp.where(odd, near, far), jnp.where(odd, far, near)


def by_partner(odd, before, after):
    near, far = jnp.where(odd, before, after), jnp.where(odd, after, before)
    return near.astype(jnp.bfloat16), far.astype(jnp.bfloat16)


def whole_rows(side_ref, near_ref, state_ref, far_ref):
    above, below = [], []
    for r in range(RAD):
        first, second = by_side(side_ref[0] != 0, near_ref[r], far_ref[r])
        above.append(first)
        below.append(second)
    return above + [state_ref[r].astype(jnp.float32) for r in range(state_ref.shape[0])] + below


def gelu_and_slope(x):
    c, a = math.sqrt(2.0 / math.pi), 0.044715
    square = x * x
    t = jnp.tanh(c * (x + a * (square * x)))
    cdf = 0.5 * (1.0 + t)
    slope = cdf + (0.5 * x) * (1.0 - t * t) * (c * (1.0 + (3.0 * a) * square))
    return x * cdf, slope


def main_kernel(
    side_ref, bands_ref, lat_near_ref, state_ref, lat_far_ref, lon_near_ref, lon_far_ref,
    mix_ref, in_ref, out_ref, cot_ref, packed_ref, hidden_ref, grad_ref, cells_ref, basis_ref,
):
    rows, cols, channels = state_ref.shape
    span = cols + 2 * WIDE
    kinds = basis_ref.shape[0]
    for r, line in enumerate(whole_rows(side_ref, lat_near_ref, state_ref, lat_far_ref)):
        left, right = by_side(side_ref[1] != 0, lon_near_ref[r], lon_far_ref[r])
        line = jnp.concatenate([left, line, right], axis=0)
        cells_ref[r * span : (r + 1) * span] = line.astype(jnp.bfloat16)
    used = (rows + 2 * RAD) * span
    cells_ref[used:] = jnp.zeros((cells_ref.shape[0] - used, channels), jnp.bfloat16)

    depth = bands_ref.shape[2]
    for i in range(rows):
        taken = dot(bands_ref[i], cells_ref[i * span : i * span + depth])
        taken = taken[: kinds * cols] + taken[kinds * cols :]
        for k in range(kinds):
            piece = taken[k * cols : (k + 1) * cols].astype(jnp.bfloat16)
            basis_ref[k, i * cols : (i + 1) * cols] = piece
    mixed = sum(dot(basis_ref[k], mix_ref[k]) for k in range(kinds)).astype(jnp.bfloat16)

    cot = cot_ref[...]
    core, half = side_ref[1], packed_ref.shape[1]

    def pack(matrix, place, height):
        for c in range(0, matrix.shape[1], LANES):
            owner, at = divmod(place + (c // LANES) * height, half)
            slot = core if owner == 0 else 1 - core
            packed_ref[slot, at : at + matrix.shape[0]] = matrix[:, c : c + LANES].astype(jnp.bfloat16)

    units = in_ref.shape[1]
    outer_at, inner_at = 0, units * (channels // LANES)
    basis_at = inner_at + channels * (units // LANES)
    back = jnp.zeros((rows * cols, channels), jnp.float32)
    for c in range(0, units, CHUNK):
        weight = in_ref[:, c : c + CHUNK]
        hidden, slope = gelu_and_slope(dot(mixed, weight))
        hidden = hidden.astype(jnp.bfloat16)
        upstream = dot(cot, out_ref[c : c + CHUNK], COLS)
        grad_pre = (upstream * slope).astype(jnp.bfloat16)
        hidden_ref[:, c : c + CHUNK] = hidden
        back = back + dot(grad_pre, weight, COLS)
        pack(dot(hidden, cot, ROWS), outer_at + c, units)
        pack(dot(mixed, grad_pre, ROWS), inner_at + (c // LANES) * channels, channels)
    grad_mixed = back.astype(jnp.bfloat16)
    grad_ref[...] = grad_mixed
    for k in range(kinds):
        pack(dot(basis_ref[k], grad_mixed, ROWS), basis_at + k * channels, kinds * channels)


def adjoint_kernel(
    side_ref, grad_ref, mix_ref, bands_ref, far_ref, near_ref, middle_ref, back_ref, landing_ref
):
    tall, cols, channels = middle_ref.shape
    rows, span = tall - 2 * RAD, cols + 2 * WIDE
    kinds = mix_ref.shape[0]
    grad = grad_ref[...]
    for k in range(kinds):
        back_ref[k] = dot(grad, mix_ref[k], COLS).astype(jnp.bfloat16)
    landing_ref[...] = jnp.zeros_like(landing_ref)
    depth = bands_ref.shape[2]
    for i in range(rows):
        pieces = [back_ref[k, i * cols : (i + 1) * cols] for k in range(kinds)]
        taken = jnp.concatenate(pieces + pieces, axis=0)
        landing_ref[i * span : i * span + depth] += dot(bands_ref[i], taken, ROWS)
    for r in range(rows + 2 * RAD):
        line = landing_ref[r * span : (r + 1) * span]
        near_ref[r], far_ref[r] = by_partner(side_ref[1] != 0, line[:WIDE], line[WIDE + cols :])
        middle_ref[r] = line[WIDE : WIDE + cols]


def rims_kernel(side_ref, middle_ref, near_ref, far_ref, to_far_ref, to_near_ref, core_ref):
    rows, cols = core_ref.shape[:2]
    lines = []
    for r in range(rows + 2 * RAD):
        left, right = by_side(side_ref[1] != 0, near_ref[r], far_ref[r])
        line = middle_ref[r]
        head, tail = line[:WIDE] + left, line[cols - WIDE :] + right
        lines.append(jnp.concatenate([head, line[WIDE : cols - WIDE], tail], axis=0))
    for r in range(RAD):
        above, below = lines[r], lines[rows + RAD + r]
        to_near_ref[r], to_far_ref[r] = by_partner(side_ref[0] != 0, above, below)
    for r in range(rows):
        core_ref[r] = lines[RAD + r]


def final_kernel(
    side_ref, hidden_ref, out_ref, state_ref, cot_ref, core_ref, near_ref, far_ref, block_ref, field_ref
):
    rows, cols = core_ref.shape[:2]
    branch = dot(hidden_ref[...], out_ref[...])
    lines = [core_ref[r] for r in range(rows)]
    for r in range(RAD):
        above, below = by_side(side_ref[0] != 0, near_ref[r], far_ref[r])
        lines[r] = lines[r] + above
        lines[rows - RAD + r] = lines[rows - RAD + r] + below
    for r in range(rows):
        at = slice(r * cols, (r + 1) * cols)
        block_ref[r] = (state_ref[r].astype(jnp.float32) + branch[at]).astype(jnp.bfloat16)
        field_ref[r] = (cot_ref[at].astype(jnp.float32) + lines[r]).astype(jnp.bfloat16)


def inner_edges_kernel(side_ref, state_ref, near_ref, far_ref):
    rows, cols = state_ref.shape[:2]
    for r in range(rows):
        line = state_ref[r].astype(jnp.float32)
        near_ref[r], far_ref[r] = by_partner(side_ref[1] != 0, line[:WIDE], line[cols - WIDE :])


def edges_kernel(side_ref, lat_near_ref, lat_far_ref, own_near_ref, own_far_ref, far_ref, near_ref):
    rows, cols = own_near_ref.shape[0], lat_near_ref.shape[1]
    near_ref[RAD : RAD + rows] = own_near_ref[...]
    far_ref[RAD : RAD + rows] = own_far_ref[...]
    for r in range(RAD):
        lines = by_side(side_ref[0] != 0, lat_near_ref[r], lat_far_ref[r])
        for at, line in zip((r, RAD + rows + r), lines):
            near_ref[at], far_ref[at] = by_partner(side_ref[1] != 0, line[:WIDE], line[cols - WIDE :])


def add_kernel(a_ref, b_ref, sum_ref):
    sum_ref[...] = (a_ref[0].astype(jnp.float32) + b_ref[...].astype(jnp.float32)).astype(jnp.bfloat16)


def tie_kernel(value_ref, *refs):
    refs[-1][...] = value_ref[...]


def tie(value, *later_than):
    return kernel_call(
        tie_kernel,
        (value, *later_than),
        [VMEM] + [ANY] * len(later_than),
        [like(value.shape, value.dtype)],
        name="tie",
    )[0]


def sum_kernel(scale, parts_ref, *refs):
    out_ref = refs[-1]
    total = parts_ref[0].astype(jnp.float32)
    for i in range(1, parts_ref.shape[0]):
        total = total + parts_ref[i].astype(jnp.float32)
    total = (total * scale).astype(out_ref.dtype)
    for i in range(out_ref.shape[0]):
        out_ref[i] = total


def sum_and_copy(parts, scale, copies, *later_than):
    return kernel_call(
        functools.partial(sum_kernel, scale),
        (parts, *later_than),
        [VMEM] + [ANY] * len(later_than),
        [like((copies,) + parts.shape[1:], jnp.bfloat16)],
        flops=parts.size,
        mib=16,
        name="sum_and_copy",
    )[0]


def runs_of(shapes, half):
    runs, start = ([], []), 0
    for out, (rows, cols) in enumerate(shapes):
        for col in range(0, cols, LANES):
            at = start
            while at < start + rows:
                which = at // half
                height = min(start + rows, (which + 1) * half) - at
                runs[which].append((out, at - start, col, at - which * half, height))
                at += height
            start += rows
    return runs


def place_kernel(runs, side_ref, mine_ref, other_ref, *outs):
    for core in range(2):

        @pl.when(side_ref[1] == core)
        def _(core=core):
            for which in range(2):
                half_ref = mine_ref if which == core else other_ref
                for out, row, col, at, height in runs[which]:
                    outs[out][row : row + height, col : col + LANES] = half_ref[at : at + height]


def swap(cells, axes, lead, closed):
    count = lax.axis_size(axes)
    pairs = []
    for i in range(lead, count, 2):
        if closed or i + 1 < count:
            pairs += [(i, (i + 1) % count), ((i + 1) % count, i)]
    return lax.ppermute(cells, axes, pairs)


def swap_both(near, far, axes, closed):
    far = swap(far, axes, 1, closed)
    return swap(near, axes, 0, closed), far


def local(
    state_field, support_offsets, kernel_values, basis_weight, weight_in, weight_out, cotangent
):
    rows, cols, channels = state_field.shape
    kinds, units = basis_weight.shape[0], weight_in.shape[1]
    grid = state_field.shape
    cells, span = rows * cols, cols + 2 * WIDE
    tall = rows + 2 * RAD
    depth = -(-LAGS * span // LANES) * LANES
    near, far = lax.axis_size(NEAR), lax.axis_size(FAR)
    cot_flat = cotangent.reshape(cells, channels)
    f32, bf16 = jnp.float32, jnp.bfloat16

    odd_lat, odd_lon = lax.axis_index(LAT) % 2, lax.axis_index(LON) % 2
    sides = jnp.stack([odd_lat, odd_lon])
    edge = like((RAD, cols, channels), bf16)
    last = rows - RAD
    to_near = lax.dynamic_slice_in_dim(state_field, jnp.where(odd_lat == 0, last, 0), RAD, 0)
    to_far = lax.dynamic_slice_in_dim(state_field, jnp.where(odd_lat == 0, 0, last), RAD, 0)
    lat_near, lat_far = swap_both(to_near, to_far, LAT, False)

    band_start = lax.axis_index(LAT) * rows
    offsets = lax.dynamic_slice_in_dim(support_offsets, band_start, rows, 0)
    values = lax.dynamic_slice_in_dim(kernel_values, band_start, rows, 1).astype(f32)
    (bands,) = kernel_call(
        functools.partial(bands_kernel, cols),
        (offsets.reshape(rows, -1), values.reshape(kinds, rows, -1)),
        [VMEM, VMEM],
        [like((rows, 2 * kinds * cols, depth), bf16)],
        [pltpu.VMEM((kinds, rows, depth), f32)],
        flops=4 * 10**9,
        name="bands",
    )
    rim = like((tall, WIDE, channels), bf16)
    own = like((rows, WIDE, channels), bf16)
    own_near, own_far = kernel_call(
        inner_edges_kernel, (sides, state_field), [SMEM, VMEM], [own, own], name="inner_edges"
    )
    to_far, to_near = kernel_call(
        edges_kernel,
        (sides, lat_near, lat_far, own_near, own_far),
        [SMEM] + [VMEM] * 4,
        [rim, rim],
        name="edges",
    )
    lon_near, lon_far = swap_both(to_near, to_far, LON, True)
    packed_rows = channels * (2 * units + kinds * channels) // LANES
    core = lax.axis_index(CORE)
    half = like((packed_rows // 2, LANES), bf16)
    packed, hidden, grad_mixed = kernel_call(
        main_kernel,
        (
            sides, bands, lat_near, state_field, lat_far, lon_near, lon_far,
            basis_weight, weight_in, weight_out, cot_flat,
        ),
        [SMEM] + [VMEM] * 10,
        [like((2,) + half.shape, bf16), like((cells, units), bf16), like((cells, channels), bf16)],
        [
            pltpu.VMEM((rows * span + depth, channels), bf16),
            pltpu.VMEM((kinds, cells, channels), bf16),
        ],
        flops=10 * cells * channels * units,
        name="main",
    )

    arrived = swap(packed[1], CORE, 0, True)
    chip = kernel_call(add_kernel, (packed, arrived), [VMEM] * 2, [half], name="add")[0]
    shares = lax.all_to_all(chip.reshape(near, -1, LANES), NEAR, 0, 0)

    to_far, to_near, middle = kernel_call(
        adjoint_kernel,
        (sides, grad_mixed, basis_weight, bands),
        [SMEM] + [VMEM] * 3,
        [rim, rim, like((tall, cols, channels), f32)],
        [
            pltpu.VMEM((kinds, cells, channels), bf16),
            pltpu.VMEM((rows * span + depth, channels), f32),
        ],
        flops=4 * cells * channels * units,
        name="adjoint",
    )
    near_rim, far_rim = swap_both(to_near, to_far, LON, True)
    planes = sum_and_copy(shares, 1.0, far, near_rim, far_rim)
    planes = lax.all_to_all(planes, FAR, 0, 0)
    to_far, to_near, inside = kernel_call(
        rims_kernel,
        (sides, middle, near_rim, far_rim),
        [SMEM] + [VMEM] * 3,
        [edge, edge, like(grid, f32)],
        name="rims",
    )
    near_edge, far_edge = swap_both(to_near, to_far, LAT, False)
    scale = 1.0 / math.sqrt(cells * lax.axis_size(LAT) * lax.axis_size(LON))
    copies = sum_and_copy(planes, scale, near, near_edge, far_edge)
    block_out, grad_field = kernel_call(
        final_kernel,
        (sides, hidden, weight_out, state_field, cot_flat, inside, near_edge, far_edge),
        [SMEM] + [VMEM] * 7,
        [like(grid, bf16), like(grid, bf16)],
        flops=2 * cells * channels * units,
        name="final",
    )
    mine = lax.all_to_all(copies, NEAR, 0, 0).reshape(-1, LANES)
    other = swap(mine, CORE, 0, True)
    shapes = ((units, channels), (channels, units), (kinds * channels, channels))
    grad_out, grad_in, grad_basis = kernel_call(
        functools.partial(place_kernel, runs_of(shapes, packed_rows // 2)),
        (sides, mine, other),
        [SMEM, VMEM, VMEM],
        [like(shape, bf16) for shape in shapes],
        name="place",
    )
    return (block_out, grad_field, grad_basis.reshape(basis_weight.shape), grad_in, grad_out)


def solution(mesh):
    names, sizes = zip(*FINE)
    mesh = Mesh(mesh.devices.reshape(sizes), names)
    return jax.shard_map(
        local,
        mesh=mesh,
        in_specs=(P(LAT, LON, None), P(), P(), P(), P(), P(), P(LAT, LON, None)),
        out_specs=(P(LAT, LON, None), P(LAT, LON, None), P(), P(), P()),
        check_vma=False,
    )
```

```python
import functools
import math

import jax
import jax.numpy as jnp
from jax import lax
from jax.experimental import pallas as pl
from jax.experimental.pallas import tpu as pltpu
from jax.sharding import Mesh
from jax.sharding import PartitionSpec as P

RAD = 2
WIDE = 8
LAGS = 2 * RAD + 1

FINE = (("z_hi", 4), ("x", 4), ("z_mid", 2), ("z_low", 2), ("y", 4), ("core", 2))
LAT = ("z_hi", "x")
LON = ("z_mid", "z_low", "y", "core")
CORE = "core"
NEAR = ("x", "z_low", "y")
FAR = ("z_hi", "z_mid")
LANES = 128
CHUNK = 256

ROWS, COLS = ((0,), (0,)), ((1,), (1,))
VMEM = pl.BlockSpec(memory_space=pltpu.VMEM)
SMEM = pl.BlockSpec(memory_space=pltpu.SMEM)
ANY = pl.BlockSpec(memory_space=pl.ANY)


def dot(a, b, contract=((1,), (0,))):
    return lax.dot_general(a, b, (contract, ((), ())), preferred_element_type=jnp.float32)


def kernel_call(
    body, operands, specs, outs, scratch=(), flops=0, mib=16, name=None, out_spec=VMEM
):
    moved = sum(x.size * x.dtype.itemsize for x in (*operands, *outs))
    return pl.pallas_call(
        body,
        out_shape=tuple(outs),
        in_specs=specs,
        out_specs=tuple(out_spec for _ in outs),
        scratch_shapes=scratch,
        compiler_params=pltpu.CompilerParams(vmem_limit_bytes=mib << 20),
        cost_estimate=pl.CostEstimate(flops=flops, bytes_accessed=moved, transcendentals=0),
        name=name,
    )(*operands)


def like(shape, dtype):
    return jax.ShapeDtypeStruct(shape, dtype)


def bands_kernel(cols, offset_ref, value_ref, bands_ref, first_ref):
    cycles, height, depth = bands_ref.shape
    kinds, span = height // (2 * cols), cols + 2 * WIDE
    slots = offset_ref.shape[1] // LAGS
    lane = lax.broadcasted_iota(jnp.int32, (cycles, LANES), 1)
    for start in range(0, depth, LANES):
        sums = [jnp.zeros((cycles, LANES), jnp.float32) for _ in range(kinds)]
        for q in range(LAGS):
            if q * span + 2 * WIDE < start or q * span >= start + LANES:
                continue
            for s in range(slots):
                at = slice(q * slots + s, q * slots + s + 1)
                hit = lane == offset_ref[:, at] + (q * span + WIDE - start)
                for k in range(kinds):
                    sums[k] = sums[k] + jnp.where(hit, value_ref[k, :, at], 0.0)
        for k in range(kinds):
            first_ref[k, :, start : start + LANES] = sums[k]
    for i in range(cycles):
        for k in range(kinds):
            block = jnp.broadcast_to(first_ref[k, i : i + 1, :], (cols, depth))
            block = pltpu.roll(block, 0, 1, stride=1, stride_axis=0)
            high = block.astype(jnp.bfloat16)
            low = (block - high.astype(jnp.float32)).astype(jnp.bfloat16)
            bands_ref[i, k * cols : (k + 1) * cols] = high
            bands_ref[i, (kinds + k) * cols : (kinds + k + 1) * cols] = low


def by_side(odd, near, far):
    near, far = near.astype(jnp.float32), far.astype(jnp.float32)
    return jnp.where(odd, near, far), jnp.where(odd, far, near)


def by_partner(odd, before, after):
    near, far = jnp.where(odd, before, after), jnp.where(odd, after, before)
    return near.astype(jnp.bfloat16), far.astype(jnp.bfloat16)


def whole_rows(side_ref, near_ref, state_ref, far_ref):
    above, below = [], []
    for r in range(RAD):
        first, second = by_side(side_ref[0] != 0, near_ref[r], far_ref[r])
        above.append(first)
        below.append(second)
    return above + [state_ref[r].astype(jnp.float32) for r in range(state_ref.shape[0])] + below


def gelu_and_slope(x):
    c, a = math.sqrt(2.0 / math.pi), 0.044715
    square = x * x
    t = jnp.tanh(c * (x + a * (square * x)))
    cdf = 0.5 * (1.0 + t)
    slope = cdf + (0.5 * x) * (1.0 - t * t) * (c * (1.0 + (3.0 * a) * square))
    return x * cdf, slope


def main_kernel(
    side_ref, bands_ref, lat_near_ref, state_ref, lat_far_ref, lon_far_ref, lon_near_ref,
    mix_ref, in_ref, out_ref, cot_ref, packed_ref, hidden_ref, grad_ref, cells_ref, basis_ref,
):
    rows, cols, channels = state_ref.shape
    span = cols + 2 * WIDE
    kinds = basis_ref.shape[0]
    for r, line in enumerate(whole_rows(side_ref, lat_near_ref, state_ref, lat_far_ref)):
        left, right = by_side(side_ref[1] != 0, lon_near_ref[r], lon_far_ref[r])
        line = jnp.concatenate([left, line, right], axis=0)
        cells_ref[r * span : (r + 1) * span] = line.astype(jnp.bfloat16)
    used = (rows + 2 * RAD) * span
    cells_ref[used:] = jnp.zeros((cells_ref.shape[0] - used, channels), jnp.bfloat16)

    depth = bands_ref.shape[2]
    for i in range(rows):
        taken = dot(bands_ref[i], cells_ref[i * span : i * span + depth])
        taken = taken[: kinds * cols] + taken[kinds * cols :]
        for k in range(kinds):
            piece = taken[k * cols : (k + 1) * cols].astype(jnp.bfloat16)
            basis_ref[k, i * cols : (i + 1) * cols] = piece
    mixed = sum(dot(basis_ref[k], mix_ref[k]) for k in range(kinds)).astype(jnp.bfloat16)

    cot = cot_ref[...]
    core, half = side_ref[1], packed_ref.shape[1]

    def pack(matrix, place, height):
        for c in range(0, matrix.shape[1], LANES):
            owner, at = divmod(place + (c // LANES) * height, half)
            slot = core if owner == 0 else 1 - core
            packed_ref[slot, at : at + matrix.shape[0]] = matrix[:, c : c + LANES].astype(jnp.bfloat16)

    units = in_ref.shape[1]
    outer_at, inner_at = 0, units * (channels // LANES)
    basis_at = inner_at + channels * (units // LANES)
    back = jnp.zeros((rows * cols, channels), jnp.float32)
    for c in range(0, units, CHUNK):
        weight = in_ref[:, c : c + CHUNK]
        hidden, slope = gelu_and_slope(dot(mixed, weight))
        hidden = hidden.astype(jnp.bfloat16)
        upstream = dot(cot, out_ref[c : c + CHUNK], COLS)
        grad_pre = (upstream * slope).astype(jnp.bfloat16)
        hidden_ref[:, c : c + CHUNK] = hidden
        back = back + dot(grad_pre, weight, COLS)
        pack(dot(hidden, cot, ROWS), outer_at + c, units)
        pack(dot(mixed, grad_pre, ROWS), inner_at + (c // LANES) * channels, channels)
    grad_mixed = back.astype(jnp.bfloat16)
    grad_ref[...] = grad_mixed
    for k in range(kinds):
        pack(dot(basis_ref[k], grad_mixed, ROWS), basis_at + k * channels, kinds * channels)


def adjoint_kernel(
    side_ref, grad_ref, mix_ref, bands_ref, far_ref, near_ref, middle_ref, back_ref, landing_ref
):
    tall, cols, channels = middle_ref.shape
    rows, span = tall - 2 * RAD, cols + 2 * WIDE
    kinds = mix_ref.shape[0]
    grad = grad_ref[...]
    for k in range(kinds):
        back_ref[k] = dot(grad, mix_ref[k], COLS).astype(jnp.bfloat16)
    landing_ref[...] = jnp.zeros_like(landing_ref)
    depth = bands_ref.shape[2]
    for i in range(rows):
        pieces = [back_ref[k, i * cols : (i + 1) * cols] for k in range(kinds)]
        taken = jnp.concatenate(pieces + pieces, axis=0)
        landing_ref[i * span : i * span + depth] += dot(bands_ref[i], taken, ROWS)
    for r in range(rows + 2 * RAD):
        line = landing_ref[r * span : (r + 1) * span]
        near_ref[r], far_ref[r] = by_partner(side_ref[1] != 0, line[:WIDE], line[WIDE + cols :])
        middle_ref[r] = line[WIDE : WIDE + cols]


def rims_kernel(side_ref, middle_ref, near_ref, far_ref, to_far_ref, to_near_ref, core_ref):
    rows, cols = core_ref.shape[:2]
    lines = []
    for r in range(rows + 2 * RAD):
        left, right = by_side(side_ref[1] != 0, near_ref[r], far_ref[r])
        line = middle_ref[r]
        head, tail = line[:WIDE] + left, line[cols - WIDE :] + right
        lines.append(jnp.concatenate([head, line[WIDE : cols - WIDE], tail], axis=0))
    for r in range(RAD):
        above, below = lines[r], lines[rows + RAD + r]
        to_near_ref[r], to_far_ref[r] = by_partner(side_ref[0] != 0, above, below)
    for r in range(rows):
        core_ref[r] = lines[RAD + r]


def final_kernel(
    side_ref, hidden_ref, out_ref, state_ref, cot_ref, core_ref, near_ref, far_ref, block_ref, field_ref
):
    rows, cols = core_ref.shape[:2]
    branch = dot(hidden_ref[...], out_ref[...])
    lines = [core_ref[r] for r in range(rows)]
    for r in range(RAD):
        above, below = by_side(side_ref[0] != 0, near_ref[r], far_ref[r])
        lines[r] = lines[r] + above
        lines[rows - RAD + r] = lines[rows - RAD + r] + below
    for r in range(rows):
        at = slice(r * cols, (r + 1) * cols)
        block_ref[r] = (state_ref[r].astype(jnp.float32) + branch[at]).astype(jnp.bfloat16)
        field_ref[r] = (cot_ref[at].astype(jnp.float32) + lines[r]).astype(jnp.bfloat16)


def inner_edges_kernel(side_ref, state_ref, near_ref, far_ref):
    rows, cols = state_ref.shape[:2]
    for r in range(rows):
        line = state_ref[r].astype(jnp.float32)
        near_ref[r], far_ref[r] = by_partner(side_ref[1] != 0, line[:WIDE], line[cols - WIDE :])


def edges_kernel(side_ref, lat_near_ref, lat_far_ref, own_near_ref, own_far_ref, far_ref, near_ref):
    rows, cols = own_near_ref.shape[0], lat_near_ref.shape[1]
    near_ref[RAD : RAD + rows] = own_near_ref[...]
    far_ref[RAD : RAD + rows] = own_far_ref[...]
    for r in range(RAD):
        lines = by_side(side_ref[0] != 0, lat_near_ref[r], lat_far_ref[r])
        for at, line in zip((r, RAD + rows + r), lines):
            near_ref[at], far_ref[at] = by_partner(side_ref[1] != 0, line[:WIDE], line[cols - WIDE :])


def add_kernel(a_ref, b_ref, later_than_ref, sum_hbm, sum_ref, sems):
    pieces = sems.shape[0]
    height = sum_ref.shape[0] // pieces
    copies = []
    for i in range(pieces):
        at = slice(i * height, (i + 1) * height)
        total = a_ref[0, at].astype(jnp.float32) + b_ref[at].astype(jnp.float32)
        sum_ref[at] = total.astype(jnp.bfloat16)
        span = pl.ds(i * height, height)
        copies.append(pltpu.make_async_copy(sum_ref.at[span], sum_hbm.at[span], sems.at[i]))
        copies[i].start()
    for copy in copies:
        copy.wait()


def tie_kernel(value_ref, *refs):
    refs[-1][...] = value_ref[...]


def tie(value, *later_than):
    return kernel_call(
        tie_kernel,
        (value, *later_than),
        [VMEM] + [ANY] * len(later_than),
        [like(value.shape, value.dtype)],
        name="tie",
    )[0]


def sum_kernel(scale, parts_ref, *refs):
    out_ref = refs[-1]
    total = parts_ref[0].astype(jnp.float32)
    for i in range(1, parts_ref.shape[0]):
        total = total + parts_ref[i].astype(jnp.float32)
    total = (total * scale).astype(out_ref.dtype)
    for i in range(out_ref.shape[0]):
        out_ref[i] = total


def sum_and_copy(parts, scale, copies, *later_than):
    return kernel_call(
        functools.partial(sum_kernel, scale),
        (parts, *later_than),
        [VMEM] + [ANY] * len(later_than),
        [like((copies,) + parts.shape[1:], jnp.bfloat16)],
        flops=parts.size,
        mib=16,
        name="sum_and_copy",
    )[0]


def runs_of(shapes, half):
    runs, start = ([], []), 0
    for out, (rows, cols) in enumerate(shapes):
        for col in range(0, cols, LANES):
            at = start
            while at < start + rows:
                which = at // half
                height = min(start + rows, (which + 1) * half) - at
                runs[which].append((out, at - start, col, at - which * half, height))
                at += height
            start += rows
    return runs


def place_kernel(runs, side_ref, mine_ref, other_ref, *refs):
    *refs, sems = refs
    count = len(refs) // 2
    outs, places = refs[:count], refs[count:]
    copies = []
    for o, place_ref in enumerate(places):
        for core in range(2):

            @pl.when(side_ref[1] == core)
            def _(core=core, o=o, place_ref=place_ref):
                for which in range(2):
                    half_ref = mine_ref if which == core else other_ref
                    for out, row, col, at, height in runs[which]:
                        if out == o:
                            place_ref[row : row + height, col : col + LANES] = half_ref[at : at + height]

        copies.append(pltpu.make_async_copy(place_ref, outs[o], sems.at[o]))
        copies[o].start()
    for copy in copies:
        copy.wait()


def swap(cells, axes, lead, closed):
    count = lax.axis_size(axes)
    pairs = []
    for i in range(lead, count, 2):
        if closed or i + 1 < count:
            pairs += [(i, (i + 1) % count), ((i + 1) % count, i)]
    return lax.ppermute(cells, axes, pairs)


def swap_both(near, far, axes, closed):
    far = swap(far, axes, 1, closed)
    return swap(near, axes, 0, closed), far


def local(
    state_field, support_offsets, kernel_values, basis_weight, weight_in, weight_out, cotangent
):
    rows, cols, channels = state_field.shape
    kinds, units = basis_weight.shape[0], weight_in.shape[1]
    grid = state_field.shape
    cells, span = rows * cols, cols + 2 * WIDE
    tall = rows + 2 * RAD
    depth = -(-LAGS * span // LANES) * LANES
    near, far = lax.axis_size(NEAR), lax.axis_size(FAR)
    cot_flat = cotangent.reshape(cells, channels)
    f32, bf16 = jnp.float32, jnp.bfloat16

    odd_lat, odd_lon = lax.axis_index(LAT) % 2, lax.axis_index(LON) % 2
    sides = jnp.stack([odd_lat, odd_lon])
    edge = like((RAD, cols, channels), bf16)
    last = rows - RAD
    to_near = lax.dynamic_slice_in_dim(state_field, jnp.where(odd_lat == 0, last, 0), RAD, 0)
    to_far = lax.dynamic_slice_in_dim(state_field, jnp.where(odd_lat == 0, 0, last), RAD, 0)
    lat_near, lat_far = swap_both(to_near, to_far, LAT, False)

    band_start = lax.axis_index(LAT) * rows
    offsets = lax.dynamic_slice_in_dim(support_offsets, band_start, rows, 0)
    values = lax.dynamic_slice_in_dim(kernel_values, band_start, rows, 1).astype(f32)
    (bands,) = kernel_call(
        functools.partial(bands_kernel, cols),
        (offsets.reshape(rows, -1), values.reshape(kinds, rows, -1)),
        [VMEM, VMEM],
        [like((rows, 2 * kinds * cols, depth), bf16)],
        [pltpu.VMEM((kinds, rows, depth), f32)],
        flops=4 * 10**9,
        name="bands",
    )
    rim = like((tall, WIDE, channels), bf16)
    own = like((rows, WIDE, channels), bf16)
    own_near, own_far = kernel_call(
        inner_edges_kernel, (sides, state_field), [SMEM, VMEM], [own, own], name="inner_edges"
    )
    to_far, to_near = kernel_call(
        edges_kernel,
        (sides, lat_near, lat_far, own_near, own_far),
        [SMEM] + [VMEM] * 4,
        [rim, rim],
        name="edges",
    )
    lon_near, lon_far = swap_both(to_near, to_far, LON, True)
    packed_rows = channels * (2 * units + kinds * channels) // LANES
    core = lax.axis_index(CORE)
    half = like((packed_rows // 2, LANES), bf16)
    packed, hidden, grad_mixed = kernel_call(
        main_kernel,
        (
            sides, bands, lat_near, state_field, lat_far, lon_far, lon_near,
            basis_weight, weight_in, weight_out, cot_flat,
        ),
        [SMEM] + [VMEM] * 10,
        [like((2,) + half.shape, bf16), like((cells, units), bf16), like((cells, channels), bf16)],
        [
            pltpu.VMEM((rows * span + depth, channels), bf16),
            pltpu.VMEM((kinds, cells, channels), bf16),
        ],
        flops=10 * cells * channels * units,
        name="main",
    )

    arrived = swap(packed[1], CORE, 0, True)
    to_far, to_near, middle = kernel_call(
        adjoint_kernel,
        (sides, grad_mixed, basis_weight, bands),
        [SMEM] + [VMEM] * 3,
        [rim, rim, like((tall, cols, channels), f32)],
        [
            pltpu.VMEM((kinds, cells, channels), bf16),
            pltpu.VMEM((rows * span + depth, channels), f32),
        ],
        flops=4 * cells * channels * units,
        name="adjoint",
    )
    chip = kernel_call(
        add_kernel,
        (packed, arrived, to_near),
        [VMEM, VMEM, ANY],
        [half],
        [pltpu.VMEM(half.shape, bf16), pltpu.SemaphoreType.DMA((4,))],
        name="add",
        out_spec=ANY,
    )[0]
    shares = lax.all_to_all(chip.reshape(near, -1, LANES), NEAR, 0, 0)

    near_rim, far_rim = swap_both(to_near, to_far, LON, True)
    planes = sum_and_copy(shares, 1.0, far, near_rim, far_rim)
    planes = lax.all_to_all(planes, FAR, 0, 0)
    to_far, to_near, inside = kernel_call(
        rims_kernel,
        (sides, middle, near_rim, far_rim),
        [SMEM] + [VMEM] * 3,
        [edge, edge, like(grid, f32)],
        name="rims",
    )
    near_edge, far_edge = swap_both(to_near, to_far, LAT, False)
    scale = 1.0 / math.sqrt(cells * lax.axis_size(LAT) * lax.axis_size(LON))
    copies = sum_and_copy(planes, scale, near, near_edge, far_edge)
    block_out, grad_field = kernel_call(
        final_kernel,
        (sides, hidden, weight_out, state_field, cot_flat, inside, near_edge, far_edge),
        [SMEM] + [VMEM] * 7,
        [like(grid, bf16), like(grid, bf16)],
        flops=2 * cells * channels * units,
        name="final",
    )
    mine = lax.all_to_all(copies, NEAR, 0, 0).reshape(-1, LANES)
    other = swap(mine, CORE, 0, True)
    shapes = ((units, channels), (channels, units), (kinds * channels, channels))
    grad_out, grad_in, grad_basis = kernel_call(
        functools.partial(place_kernel, runs_of(shapes, packed_rows // 2)),
        (sides, mine, other),
        [SMEM, VMEM, VMEM],
        [like(shape, bf16) for shape in shapes],
        [*(pltpu.VMEM(shape, bf16) for shape in shapes), pltpu.SemaphoreType.DMA((3,))],
        name="place",
        out_spec=ANY,
    )
    return (block_out, grad_field, grad_basis.reshape(basis_weight.shape), grad_in, grad_out)


def solution(mesh):
    names, sizes = zip(*FINE)
    mesh = Mesh(mesh.devices.reshape(sizes), names)
    return jax.shard_map(
        local,
        mesh=mesh,
        in_specs=(P(LAT, LON, None), P(), P(), P(), P(), P(), P(LAT, LON, None)),
        out_specs=(P(LAT, LON, None), P(LAT, LON, None), P(), P(), P()),
        check_vma=False,
    )
```

```python
import functools
import math

import jax
import jax.numpy as jnp
from jax import lax
from jax.experimental import pallas as pl
from jax.experimental.pallas import tpu as pltpu
from jax.sharding import Mesh
from jax.sharding import PartitionSpec as P

RAD = 2
WIDE = 8
LAGS = 2 * RAD + 1

FINE = (("z_hi", 4), ("x", 4), ("z_mid", 2), ("z_low", 2), ("y", 4), ("core", 2))
LAT = ("z_hi", "x")
LON = ("z_mid", "z_low", "y", "core")
CORE = "core"
NEAR = ("x", "z_low", "y")
FAR = ("z_hi", "z_mid")
LANES = 128
CHUNK = 1024

ROWS, COLS = ((0,), (0,)), ((1,), (1,))
VMEM = pl.BlockSpec(memory_space=pltpu.VMEM)
SMEM = pl.BlockSpec(memory_space=pltpu.SMEM)
ANY = pl.BlockSpec(memory_space=pl.ANY)


def dot(a, b, contract=((1,), (0,))):
    return lax.dot_general(a, b, (contract, ((), ())), preferred_element_type=jnp.float32)


def kernel_call(
    body, operands, specs, outs, scratch=(), flops=0, mib=16, name=None, out_spec=VMEM
):
    moved = sum(x.size * x.dtype.itemsize for x in (*operands, *outs))
    return pl.pallas_call(
        body,
        out_shape=tuple(outs),
        in_specs=specs,
        out_specs=tuple(out_spec for _ in outs),
        scratch_shapes=scratch,
        compiler_params=pltpu.CompilerParams(vmem_limit_bytes=mib << 20),
        cost_estimate=pl.CostEstimate(flops=flops, bytes_accessed=moved, transcendentals=0),
        name=name,
    )(*operands)


def like(shape, dtype):
    return jax.ShapeDtypeStruct(shape, dtype)


def bands_kernel(cols, offset_ref, value_ref, bands_ref, first_ref):
    cycles, height, depth = bands_ref.shape
    kinds, span = height // (2 * cols), cols + 2 * WIDE
    slots = offset_ref.shape[1] // LAGS
    lane = lax.broadcasted_iota(jnp.int32, (cycles, LANES), 1)
    for start in range(0, depth, LANES):
        sums = [jnp.zeros((cycles, LANES), jnp.float32) for _ in range(kinds)]
        for q in range(LAGS):
            if q * span + 2 * WIDE < start or q * span >= start + LANES:
                continue
            for s in range(slots):
                at = slice(q * slots + s, q * slots + s + 1)
                hit = lane == offset_ref[:, at] + (q * span + WIDE - start)
                for k in range(kinds):
                    sums[k] = sums[k] + jnp.where(hit, value_ref[k, :, at], 0.0)
        for k in range(kinds):
            first_ref[k, :, start : start + LANES] = sums[k]
    for i in range(cycles):
        for k in range(kinds):
            block = jnp.broadcast_to(first_ref[k, i : i + 1, :], (cols, depth))
            block = pltpu.roll(block, 0, 1, stride=1, stride_axis=0)
            high = block.astype(jnp.bfloat16)
            low = (block - high.astype(jnp.float32)).astype(jnp.bfloat16)
            bands_ref[i, k * cols : (k + 1) * cols] = high
            bands_ref[i, (kinds + k) * cols : (kinds + k + 1) * cols] = low


def by_side(odd, near, far):
    near, far = near.astype(jnp.float32), far.astype(jnp.float32)
    return jnp.where(odd, near, far), jnp.where(odd, far, near)


def by_partner(odd, before, after):
    near, far = jnp.where(odd, before, after), jnp.where(odd, after, before)
    return near.astype(jnp.bfloat16), far.astype(jnp.bfloat16)


def whole_rows(side_ref, near_ref, state_ref, far_ref):
    above, below = [], []
    for r in range(RAD):
        first, second = by_side(side_ref[0] != 0, near_ref[r], far_ref[r])
        above.append(first)
        below.append(second)
    return above + [state_ref[r].astype(jnp.float32) for r in range(state_ref.shape[0])] + below


def gelu_and_slope(x):
    c, a = math.sqrt(2.0 / math.pi), 0.044715
    square = x * x
    t = jnp.tanh(c * (x + a * (square * x)))
    cdf = 0.5 * (1.0 + t)
    slope = cdf + (0.5 * x) * (1.0 - t * t) * (c * (1.0 + (3.0 * a) * square))
    return x * cdf, slope


def main_kernel(
    side_ref, bands_ref, lat_near_ref, state_ref, lat_far_ref, lon_far_ref, lon_near_ref,
    mix_ref, in_ref, out_ref, cot_ref, packed_ref, hidden_ref, grad_ref, cells_ref, basis_ref,
):
    rows, cols, channels = state_ref.shape
    span = cols + 2 * WIDE
    kinds = basis_ref.shape[0]
    for r, line in enumerate(whole_rows(side_ref, lat_near_ref, state_ref, lat_far_ref)):
        left, right = by_side(side_ref[1] != 0, lon_near_ref[r], lon_far_ref[r])
        line = jnp.concatenate([left, line, right], axis=0)
        cells_ref[r * span : (r + 1) * span] = line.astype(jnp.bfloat16)
    used = (rows + 2 * RAD) * span
    cells_ref[used:] = jnp.zeros((cells_ref.shape[0] - used, channels), jnp.bfloat16)

    depth = bands_ref.shape[2]
    for i in range(rows):
        taken = dot(bands_ref[i], cells_ref[i * span : i * span + depth])
        taken = taken[: kinds * cols] + taken[kinds * cols :]
        for k in range(kinds):
            piece = taken[k * cols : (k + 1) * cols].astype(jnp.bfloat16)
            basis_ref[k, i * cols : (i + 1) * cols] = piece
    mixed = sum(dot(basis_ref[k], mix_ref[k]) for k in range(kinds)).astype(jnp.bfloat16)

    cot = cot_ref[...]
    core, half = side_ref[1], packed_ref.shape[1]

    def pack(matrix, place, height):
        for c in range(0, matrix.shape[1], LANES):
            owner, at = divmod(place + (c // LANES) * height, half)
            slot = core if owner == 0 else 1 - core
            packed_ref[slot, at : at + matrix.shape[0]] = matrix[:, c : c + LANES].astype(jnp.bfloat16)

    units = in_ref.shape[1]
    outer_at, inner_at = 0, units * (channels // LANES)
    basis_at = inner_at + channels * (units // LANES)
    back = jnp.zeros((rows * cols, channels), jnp.float32)
    for c in range(0, units, CHUNK):
        weight = in_ref[:, c : c + CHUNK]
        hidden, slope = gelu_and_slope(dot(mixed, weight))
        hidden = hidden.astype(jnp.bfloat16)
        upstream = dot(cot, out_ref[c : c + CHUNK], COLS)
        grad_pre = (upstream * slope).astype(jnp.bfloat16)
        hidden_ref[:, c : c + CHUNK] = hidden
        back = back + dot(grad_pre, weight, COLS)
        pack(dot(hidden, cot, ROWS), outer_at + c, units)
        pack(dot(mixed, grad_pre, ROWS), inner_at + (c // LANES) * channels, channels)
    grad_mixed = back.astype(jnp.bfloat16)
    grad_ref[...] = grad_mixed
    for k in range(kinds):
        pack(dot(basis_ref[k], grad_mixed, ROWS), basis_at + k * channels, kinds * channels)


def adjoint_kernel(
    side_ref, grad_ref, mix_ref, bands_ref, far_ref, near_ref, middle_ref, back_ref, landing_ref
):
    tall, cols, channels = middle_ref.shape
    rows, span = tall - 2 * RAD, cols + 2 * WIDE
    kinds = mix_ref.shape[0]
    grad = grad_ref[...]
    for k in range(kinds):
        back_ref[k] = dot(grad, mix_ref[k], COLS).astype(jnp.bfloat16)
    landing_ref[...] = jnp.zeros_like(landing_ref)
    depth = bands_ref.shape[2]
    for i in range(rows):
        pieces = [back_ref[k, i * cols : (i + 1) * cols] for k in range(kinds)]
        taken = jnp.concatenate(pieces + pieces, axis=0)
        landing_ref[i * span : i * span + depth] += dot(bands_ref[i], taken, ROWS)
    for r in range(rows + 2 * RAD):
        line = landing_ref[r * span : (r + 1) * span]
        near_ref[r], far_ref[r] = by_partner(side_ref[1] != 0, line[:WIDE], line[WIDE + cols :])
        middle_ref[r] = line[WIDE : WIDE + cols]


def rims_kernel(side_ref, middle_ref, near_ref, far_ref, to_far_ref, to_near_ref, core_ref):
    rows, cols = core_ref.shape[:2]
    lines = []
    for r in range(rows + 2 * RAD):
        left, right = by_side(side_ref[1] != 0, near_ref[r], far_ref[r])
        line = middle_ref[r]
        head, tail = line[:WIDE] + left, line[cols - WIDE :] + right
        lines.append(jnp.concatenate([head, line[WIDE : cols - WIDE], tail], axis=0))
    for r in range(RAD):
        above, below = lines[r], lines[rows + RAD + r]
        to_near_ref[r], to_far_ref[r] = by_partner(side_ref[0] != 0, above, below)
    for r in range(rows):
        core_ref[r] = lines[RAD + r]


def final_kernel(
    side_ref, hidden_ref, out_ref, state_ref, cot_ref, core_ref, near_ref, far_ref, block_ref, field_ref
):
    rows, cols = core_ref.shape[:2]
    branch = dot(hidden_ref[...], out_ref[...])
    lines = [core_ref[r] for r in range(rows)]
    for r in range(RAD):
        above, below = by_side(side_ref[0] != 0, near_ref[r], far_ref[r])
        lines[r] = lines[r] + above
        lines[rows - RAD + r] = lines[rows - RAD + r] + below
    for r in range(rows):
        at = slice(r * cols, (r + 1) * cols)
        block_ref[r] = (state_ref[r].astype(jnp.float32) + branch[at]).astype(jnp.bfloat16)
        field_ref[r] = (cot_ref[at].astype(jnp.float32) + lines[r]).astype(jnp.bfloat16)


def inner_edges_kernel(side_ref, state_ref, near_ref, far_ref):
    rows, cols = state_ref.shape[:2]
    for r in range(rows):
        line = state_ref[r].astype(jnp.float32)
        near_ref[r], far_ref[r] = by_partner(side_ref[1] != 0, line[:WIDE], line[cols - WIDE :])


def edges_kernel(side_ref, lat_near_ref, lat_far_ref, own_near_ref, own_far_ref, far_ref, near_ref):
    rows, cols = own_near_ref.shape[0], lat_near_ref.shape[1]
    near_ref[RAD : RAD + rows] = own_near_ref[...]
    far_ref[RAD : RAD + rows] = own_far_ref[...]
    for r in range(RAD):
        lines = by_side(side_ref[0] != 0, lat_near_ref[r], lat_far_ref[r])
        for at, line in zip((r, RAD + rows + r), lines):
            near_ref[at], far_ref[at] = by_partner(side_ref[1] != 0, line[:WIDE], line[cols - WIDE :])


def add_kernel(a_ref, b_ref, later_than_ref, sum_hbm, sum_ref, sems):
    pieces = sems.shape[0]
    height = sum_ref.shape[0] // pieces
    copies = []
    for i in range(pieces):
        at = slice(i * height, (i + 1) * height)
        total = a_ref[0, at].astype(jnp.float32) + b_ref[at].astype(jnp.float32)
        sum_ref[at] = total.astype(jnp.bfloat16)
        span = pl.ds(i * height, height)
        copies.append(pltpu.make_async_copy(sum_ref.at[span], sum_hbm.at[span], sems.at[i]))
        copies[i].start()
    for copy in copies:
        copy.wait()


def tie_kernel(value_ref, *refs):
    refs[-1][...] = value_ref[...]


def tie(value, *later_than):
    return kernel_call(
        tie_kernel,
        (value, *later_than),
        [VMEM] + [ANY] * len(later_than),
        [like(value.shape, value.dtype)],
        name="tie",
    )[0]


def sum_kernel(scale, parts_ref, *refs):
    out_ref = refs[-1]
    total = parts_ref[0].astype(jnp.float32)
    for i in range(1, parts_ref.shape[0]):
        total = total + parts_ref[i].astype(jnp.float32)
    total = (total * scale).astype(out_ref.dtype)
    for i in range(out_ref.shape[0]):
        out_ref[i] = total


def sum_and_copy(parts, scale, copies, *later_than):
    return kernel_call(
        functools.partial(sum_kernel, scale),
        (parts, *later_than),
        [VMEM] + [ANY] * len(later_than),
        [like((copies,) + parts.shape[1:], jnp.bfloat16)],
        flops=parts.size,
        mib=16,
        name="sum_and_copy",
    )[0]


def runs_of(shapes, half):
    runs, start = ([], []), 0
    for out, (rows, cols) in enumerate(shapes):
        for col in range(0, cols, LANES):
            at = start
            while at < start + rows:
                which = at // half
                height = min(start + rows, (which + 1) * half) - at
                runs[which].append((out, at - start, col, at - which * half, height))
                at += height
            start += rows
    return runs


def place_kernel(runs, side_ref, mine_ref, other_ref, *refs):
    *refs, sems = refs
    count = len(refs) // 2
    outs, places = refs[:count], refs[count:]
    copies = []
    for o, place_ref in enumerate(places):
        for core in range(2):

            @pl.when(side_ref[1] == core)
            def _(core=core, o=o, place_ref=place_ref):
                for which in range(2):
                    half_ref = mine_ref if which == core else other_ref
                    for out, row, col, at, height in runs[which]:
                        if out == o:
                            place_ref[row : row + height, col : col + LANES] = half_ref[at : at + height]

        copies.append(pltpu.make_async_copy(place_ref, outs[o], sems.at[o]))
        copies[o].start()
    for copy in copies:
        copy.wait()


def swap(cells, axes, lead, closed):
    count = lax.axis_size(axes)
    pairs = []
    for i in range(lead, count, 2):
        if closed or i + 1 < count:
            pairs += [(i, (i + 1) % count), ((i + 1) % count, i)]
    return lax.ppermute(cells, axes, pairs)


def swap_both(near, far, axes, closed):
    far = swap(far, axes, 1, closed)
    return swap(near, axes, 0, closed), far


def local(
    state_field, support_offsets, kernel_values, basis_weight, weight_in, weight_out, cotangent
):
    rows, cols, channels = state_field.shape
    kinds, units = basis_weight.shape[0], weight_in.shape[1]
    grid = state_field.shape
    cells, span = rows * cols, cols + 2 * WIDE
    tall = rows + 2 * RAD
    depth = -(-LAGS * span // LANES) * LANES
    near, far = lax.axis_size(NEAR), lax.axis_size(FAR)
    cot_flat = cotangent.reshape(cells, channels)
    f32, bf16 = jnp.float32, jnp.bfloat16

    odd_lat, odd_lon = lax.axis_index(LAT) % 2, lax.axis_index(LON) % 2
    sides = jnp.stack([odd_lat, odd_lon])
    edge = like((RAD, cols, channels), bf16)
    last = rows - RAD
    to_near = lax.dynamic_slice_in_dim(state_field, jnp.where(odd_lat == 0, last, 0), RAD, 0)
    to_far = lax.dynamic_slice_in_dim(state_field, jnp.where(odd_lat == 0, 0, last), RAD, 0)
    lat_near, lat_far = swap_both(to_near, to_far, LAT, False)

    band_start = lax.axis_index(LAT) * rows
    offsets = lax.dynamic_slice_in_dim(support_offsets, band_start, rows, 0)
    values = lax.dynamic_slice_in_dim(kernel_values, band_start, rows, 1).astype(f32)
    (bands,) = kernel_call(
        functools.partial(bands_kernel, cols),
        (offsets.reshape(rows, -1), values.reshape(kinds, rows, -1)),
        [VMEM, VMEM],
        [like((rows, 2 * kinds * cols, depth), bf16)],
        [pltpu.VMEM((kinds, rows, depth), f32)],
        flops=4 * 10**9,
        name="bands",
    )
    rim = like((tall, WIDE, channels), bf16)
    own = like((rows, WIDE, channels), bf16)
    own_near, own_far = kernel_call(
        inner_edges_kernel, (sides, state_field), [SMEM, VMEM], [own, own], name="inner_edges"
    )
    to_far, to_near = kernel_call(
        edges_kernel,
        (sides, lat_near, lat_far, own_near, own_far),
        [SMEM] + [VMEM] * 4,
        [rim, rim],
        name="edges",
    )
    lon_near, lon_far = swap_both(to_near, to_far, LON, True)
    packed_rows = channels * (2 * units + kinds * channels) // LANES
    core = lax.axis_index(CORE)
    half = like((packed_rows // 2, LANES), bf16)
    packed, hidden, grad_mixed = kernel_call(
        main_kernel,
        (
            sides, bands, lat_near, state_field, lat_far, lon_far, lon_near,
            basis_weight, weight_in, weight_out, cot_flat,
        ),
        [SMEM] + [VMEM] * 10,
        [like((2,) + half.shape, bf16), like((cells, units), bf16), like((cells, channels), bf16)],
        [
            pltpu.VMEM((rows * span + depth, channels), bf16),
            pltpu.VMEM((kinds, cells, channels), bf16),
        ],
        flops=10 * cells * channels * units,
        name="main",
    )

    arrived = swap(packed[1], CORE, 0, True)
    to_far, to_near, middle = kernel_call(
        adjoint_kernel,
        (sides, grad_mixed, basis_weight, bands),
        [SMEM] + [VMEM] * 3,
        [rim, rim, like((tall, cols, channels), f32)],
        [
            pltpu.VMEM((kinds, cells, channels), bf16),
            pltpu.VMEM((rows * span + depth, channels), f32),
        ],
        flops=4 * cells * channels * units,
        name="adjoint",
    )
    chip = kernel_call(
        add_kernel,
        (packed, arrived, to_near),
        [VMEM, VMEM, ANY],
        [half],
        [pltpu.VMEM(half.shape, bf16), pltpu.SemaphoreType.DMA((4,))],
        name="add",
        out_spec=ANY,
    )[0]
    shares = lax.all_to_all(chip.reshape(near, -1, LANES), NEAR, 0, 0)

    near_rim, far_rim = swap_both(to_near, to_far, LON, True)
    planes = sum_and_copy(shares, 1.0, far, near_rim, far_rim)
    planes = lax.all_to_all(planes, FAR, 0, 0)
    to_far, to_near, inside = kernel_call(
        rims_kernel,
        (sides, middle, near_rim, far_rim),
        [SMEM] + [VMEM] * 3,
        [edge, edge, like(grid, f32)],
        name="rims",
    )
    near_edge, far_edge = swap_both(to_near, to_far, LAT, False)
    scale = 1.0 / math.sqrt(cells * lax.axis_size(LAT) * lax.axis_size(LON))
    copies = sum_and_copy(planes, scale, near, near_edge, far_edge)
    block_out, grad_field = kernel_call(
        final_kernel,
        (sides, hidden, weight_out, state_field, cot_flat, inside, near_edge, far_edge),
        [SMEM] + [VMEM] * 7,
        [like(grid, bf16), like(grid, bf16)],
        flops=2 * cells * channels * units,
        name="final",
    )
    mine = lax.all_to_all(copies, NEAR, 0, 0).reshape(-1, LANES)
    other = swap(mine, CORE, 0, True)
    shapes = ((units, channels), (channels, units), (kinds * channels, channels))
    grad_out, grad_in, grad_basis = kernel_call(
        functools.partial(place_kernel, runs_of(shapes, packed_rows // 2)),
        (sides, mine, other),
        [SMEM, VMEM, VMEM],
        [like(shape, bf16) for shape in shapes],
        [*(pltpu.VMEM(shape, bf16) for shape in shapes), pltpu.SemaphoreType.DMA((3,))],
        name="place",
        out_spec=ANY,
    )
    return (block_out, grad_field, grad_basis.reshape(basis_weight.shape), grad_in, grad_out)


def solution(mesh):
    names, sizes = zip(*FINE)
    mesh = Mesh(mesh.devices.reshape(sizes), names)
    return jax.shard_map(
        local,
        mesh=mesh,
        in_specs=(P(LAT, LON, None), P(), P(), P(), P(), P(), P(LAT, LON, None)),
        out_specs=(P(LAT, LON, None), P(LAT, LON, None), P(), P(), P()),
        check_vma=False,
    )
```

```python
import functools
import math

import jax
import jax.numpy as jnp
from jax import lax
from jax.experimental import pallas as pl
from jax.experimental.pallas import tpu as pltpu
from jax.sharding import Mesh
from jax.sharding import PartitionSpec as P

RAD = 2
WIDE = 8
LAGS = 2 * RAD + 1

FINE = (("z_hi", 4), ("x", 4), ("z_mid", 2), ("z_low", 2), ("y", 4), ("core", 2))
LAT = ("z_hi", "x")
LON = ("z_mid", "z_low", "y", "core")
CORE = "core"
NEAR = ("x", "z_low", "y")
FAR = ("z_hi", "z_mid")
LANES = 128
CHUNK = 1024

ROWS, COLS = ((0,), (0,)), ((1,), (1,))
VMEM = pl.BlockSpec(memory_space=pltpu.VMEM)
SMEM = pl.BlockSpec(memory_space=pltpu.SMEM)
ANY = pl.BlockSpec(memory_space=pl.ANY)


def dot(a, b, contract=((1,), (0,))):
    return lax.dot_general(a, b, (contract, ((), ())), preferred_element_type=jnp.float32)


def kernel_call(
    body, operands, specs, outs, scratch=(), flops=0, mib=40, name=None, out_spec=VMEM
):
    moved = sum(x.size * x.dtype.itemsize for x in (*operands, *outs))
    return pl.pallas_call(
        body,
        out_shape=tuple(outs),
        in_specs=specs,
        out_specs=tuple(out_spec for _ in outs),
        scratch_shapes=scratch,
        compiler_params=pltpu.CompilerParams(vmem_limit_bytes=mib << 20),
        cost_estimate=pl.CostEstimate(flops=flops, bytes_accessed=moved, transcendentals=0),
        name=name,
    )(*operands)


def like(shape, dtype):
    return jax.ShapeDtypeStruct(shape, dtype)


def bands_kernel(cols, offset_ref, value_ref, bands_ref, first_ref):
    cycles, height, depth = bands_ref.shape
    kinds, span = height // (2 * cols), cols + 2 * WIDE
    slots = offset_ref.shape[1] // LAGS
    lane = lax.broadcasted_iota(jnp.int32, (cycles, LANES), 1)
    for start in range(0, depth, LANES):
        sums = [jnp.zeros((cycles, LANES), jnp.float32) for _ in range(kinds)]
        for q in range(LAGS):
            if q * span + 2 * WIDE < start or q * span >= start + LANES:
                continue
            for s in range(slots):
                at = slice(q * slots + s, q * slots + s + 1)
                hit = lane == offset_ref[:, at] + (q * span + WIDE - start)
                for k in range(kinds):
                    sums[k] = sums[k] + jnp.where(hit, value_ref[k, :, at], 0.0)
        for k in range(kinds):
            first_ref[k, :, start : start + LANES] = sums[k]
    for i in range(cycles):
        for k in range(kinds):
            block = jnp.broadcast_to(first_ref[k, i : i + 1, :], (cols, depth))
            block = pltpu.roll(block, 0, 1, stride=1, stride_axis=0)
            high = block.astype(jnp.bfloat16)
            low = (block - high.astype(jnp.float32)).astype(jnp.bfloat16)
            bands_ref[i, k * cols : (k + 1) * cols] = high
            bands_ref[i, (kinds + k) * cols : (kinds + k + 1) * cols] = low


def by_side(odd, near, far):
    near, far = near.astype(jnp.float32), far.astype(jnp.float32)
    return jnp.where(odd, near, far), jnp.where(odd, far, near)


def by_partner(odd, before, after):
    near, far = jnp.where(odd, before, after), jnp.where(odd, after, before)
    return near.astype(jnp.bfloat16), far.astype(jnp.bfloat16)


def whole_rows(side_ref, near_ref, state_ref, far_ref):
    above, below = [], []
    for r in range(RAD):
        first, second = by_side(side_ref[0] != 0, near_ref[r], far_ref[r])
        above.append(first)
        below.append(second)
    return above + [state_ref[r].astype(jnp.float32) for r in range(state_ref.shape[0])] + below


def gelu_and_slope(x):
    c, a = math.sqrt(2.0 / math.pi), 0.044715
    square = x * x
    t = jnp.tanh(c * (x + a * (square * x)))
    cdf = 0.5 * (1.0 + t)
    slope = cdf + (0.5 * x) * (1.0 - t * t) * (c * (1.0 + (3.0 * a) * square))
    return x * cdf, slope


def main_kernel(
    side_ref, bands_ref, lat_near_ref, state_ref, lat_far_ref, lon_far_ref, lon_near_ref,
    mix_ref, in_ref, out_ref, cot_ref, packed_ref, hidden_ref, grad_ref, cells_ref, basis_ref,
):
    rows, cols, channels = state_ref.shape
    span = cols + 2 * WIDE
    kinds = basis_ref.shape[0]
    for r, line in enumerate(whole_rows(side_ref, lat_near_ref, state_ref, lat_far_ref)):
        left, right = by_side(side_ref[1] != 0, lon_near_ref[r], lon_far_ref[r])
        line = jnp.concatenate([left, line, right], axis=0)
        cells_ref[r * span : (r + 1) * span] = line.astype(jnp.bfloat16)
    used = (rows + 2 * RAD) * span
    cells_ref[used:] = jnp.zeros((cells_ref.shape[0] - used, channels), jnp.bfloat16)

    depth = bands_ref.shape[2]
    for i in range(rows):
        taken = dot(bands_ref[i], cells_ref[i * span : i * span + depth])
        taken = taken[: kinds * cols] + taken[kinds * cols :]
        for k in range(kinds):
            piece = taken[k * cols : (k + 1) * cols].astype(jnp.bfloat16)
            basis_ref[k, i * cols : (i + 1) * cols] = piece
    mixed = sum(dot(basis_ref[k], mix_ref[k]) for k in range(kinds)).astype(jnp.bfloat16)

    cot = cot_ref[...]
    core, half = side_ref[1], packed_ref.shape[1]

    def pack(matrix, place, height):
        for c in range(0, matrix.shape[1], LANES):
            owner, at = divmod(place + (c // LANES) * height, half)
            slot = core if owner == 0 else 1 - core
            packed_ref[slot, at : at + matrix.shape[0]] = matrix[:, c : c + LANES].astype(jnp.bfloat16)

    units = in_ref.shape[1]
    outer_at, inner_at = 0, units * (channels // LANES)
    basis_at = inner_at + channels * (units // LANES)
    back = jnp.zeros((rows * cols, channels), jnp.float32)
    for c in range(0, units, CHUNK):
        weight = in_ref[:, c : c + CHUNK]
        hidden, slope = gelu_and_slope(dot(mixed, weight))
        hidden = hidden.astype(jnp.bfloat16)
        upstream = dot(cot, out_ref[c : c + CHUNK], COLS)
        grad_pre = (upstream * slope).astype(jnp.bfloat16)
        hidden_ref[:, c : c + CHUNK] = hidden
        back = back + dot(grad_pre, weight, COLS)
        pack(dot(hidden, cot, ROWS), outer_at + c, units)
        pack(dot(mixed, grad_pre, ROWS), inner_at + (c // LANES) * channels, channels)
    grad_mixed = back.astype(jnp.bfloat16)
    grad_ref[...] = grad_mixed
    for k in range(kinds):
        pack(dot(basis_ref[k], grad_mixed, ROWS), basis_at + k * channels, kinds * channels)


def adjoint_kernel(
    side_ref, grad_ref, mix_ref, bands_ref, far_ref, near_ref, middle_ref, back_ref, landing_ref
):
    tall, cols, channels = middle_ref.shape
    rows, span = tall - 2 * RAD, cols + 2 * WIDE
    kinds = mix_ref.shape[0]
    grad = grad_ref[...]
    for k in range(kinds):
        back_ref[k] = dot(grad, mix_ref[k], COLS).astype(jnp.bfloat16)
    landing_ref[...] = jnp.zeros_like(landing_ref)
    depth = bands_ref.shape[2]
    for i in range(rows):
        pieces = [back_ref[k, i * cols : (i + 1) * cols] for k in range(kinds)]
        taken = jnp.concatenate(pieces + pieces, axis=0)
        landing_ref[i * span : i * span + depth] += dot(bands_ref[i], taken, ROWS)
    for r in range(rows + 2 * RAD):
        line = landing_ref[r * span : (r + 1) * span]
        near_ref[r], far_ref[r] = by_partner(side_ref[1] != 0, line[:WIDE], line[WIDE + cols :])
        middle_ref[r] = line[WIDE : WIDE + cols]


def rims_kernel(side_ref, middle_ref, near_ref, far_ref, to_far_ref, to_near_ref, core_ref):
    rows, cols = core_ref.shape[:2]
    lines = []
    for r in range(rows + 2 * RAD):
        left, right = by_side(side_ref[1] != 0, near_ref[r], far_ref[r])
        line = middle_ref[r]
        head, tail = line[:WIDE] + left, line[cols - WIDE :] + right
        lines.append(jnp.concatenate([head, line[WIDE : cols - WIDE], tail], axis=0))
    for r in range(RAD):
        above, below = lines[r], lines[rows + RAD + r]
        to_near_ref[r], to_far_ref[r] = by_partner(side_ref[0] != 0, above, below)
    for r in range(rows):
        core_ref[r] = lines[RAD + r]


def final_kernel(
    side_ref, hidden_ref, out_ref, state_ref, cot_ref, core_ref, near_ref, far_ref, block_ref, field_ref
):
    rows, cols = core_ref.shape[:2]
    branch = dot(hidden_ref[...], out_ref[...])
    lines = [core_ref[r] for r in range(rows)]
    for r in range(RAD):
        above, below = by_side(side_ref[0] != 0, near_ref[r], far_ref[r])
        lines[r] = lines[r] + above
        lines[rows - RAD + r] = lines[rows - RAD + r] + below
    for r in range(rows):
        at = slice(r * cols, (r + 1) * cols)
        block_ref[r] = (state_ref[r].astype(jnp.float32) + branch[at]).astype(jnp.bfloat16)
        field_ref[r] = (cot_ref[at].astype(jnp.float32) + lines[r]).astype(jnp.bfloat16)


def inner_edges_kernel(side_ref, state_ref, near_ref, far_ref):
    rows, cols = state_ref.shape[:2]
    for r in range(rows):
        line = state_ref[r].astype(jnp.float32)
        near_ref[r], far_ref[r] = by_partner(side_ref[1] != 0, line[:WIDE], line[cols - WIDE :])


def edges_kernel(side_ref, lat_near_ref, lat_far_ref, own_near_ref, own_far_ref, far_ref, near_ref):
    rows, cols = own_near_ref.shape[0], lat_near_ref.shape[1]
    near_ref[RAD : RAD + rows] = own_near_ref[...]
    far_ref[RAD : RAD + rows] = own_far_ref[...]
    for r in range(RAD):
        lines = by_side(side_ref[0] != 0, lat_near_ref[r], lat_far_ref[r])
        for at, line in zip((r, RAD + rows + r), lines):
            near_ref[at], far_ref[at] = by_partner(side_ref[1] != 0, line[:WIDE], line[cols - WIDE :])


def add_kernel(a_ref, b_ref, later_than_ref, sum_hbm, sum_ref, sems):
    pieces = sems.shape[0]
    height = sum_ref.shape[0] // pieces
    copies = []
    for i in range(pieces):
        at = slice(i * height, (i + 1) * height)
        total = a_ref[0, at].astype(jnp.float32) + b_ref[at].astype(jnp.float32)
        sum_ref[at] = total.astype(jnp.bfloat16)
        span = pl.ds(i * height, height)
        copies.append(pltpu.make_async_copy(sum_ref.at[span], sum_hbm.at[span], sems.at[i]))
        copies[i].start()
    for copy in copies:
        copy.wait()


def tie_kernel(value_ref, *refs):
    refs[-1][...] = value_ref[...]


def tie(value, *later_than):
    return kernel_call(
        tie_kernel,
        (value, *later_than),
        [VMEM] + [ANY] * len(later_than),
        [like(value.shape, value.dtype)],
        name="tie",
    )[0]


def sum_kernel(scale, parts_ref, *refs):
    out_ref = refs[-1]
    total = parts_ref[0].astype(jnp.float32)
    for i in range(1, parts_ref.shape[0]):
        total = total + parts_ref[i].astype(jnp.float32)
    total = (total * scale).astype(out_ref.dtype)
    for i in range(out_ref.shape[0]):
        out_ref[i] = total


def sum_and_copy(parts, scale, copies, *later_than):
    return kernel_call(
        functools.partial(sum_kernel, scale),
        (parts, *later_than),
        [VMEM] + [ANY] * len(later_than),
        [like((copies,) + parts.shape[1:], jnp.bfloat16)],
        flops=parts.size,
        mib=40,
        name="sum_and_copy",
    )[0]


def runs_of(shapes, half):
    runs, start = ([], []), 0
    for out, (rows, cols) in enumerate(shapes):
        for col in range(0, cols, LANES):
            at = start
            while at < start + rows:
                which = at // half
                height = min(start + rows, (which + 1) * half) - at
                runs[which].append((out, at - start, col, at - which * half, height))
                at += height
            start += rows
    return runs


def place_kernel(runs, side_ref, mine_ref, other_ref, *refs):
    *refs, sems = refs
    count = len(refs) // 2
    outs, places = refs[:count], refs[count:]
    copies = []
    for o, place_ref in enumerate(places):
        for core in range(2):

            @pl.when(side_ref[1] == core)
            def _(core=core, o=o, place_ref=place_ref):
                for which in range(2):
                    half_ref = mine_ref if which == core else other_ref
                    for out, row, col, at, height in runs[which]:
                        if out == o:
                            place_ref[row : row + height, col : col + LANES] = half_ref[at : at + height]

        copies.append(pltpu.make_async_copy(place_ref, outs[o], sems.at[o]))
        copies[o].start()
    for copy in copies:
        copy.wait()


def swap(cells, axes, lead, closed):
    count = lax.axis_size(axes)
    pairs = []
    for i in range(lead, count, 2):
        if closed or i + 1 < count:
            pairs += [(i, (i + 1) % count), ((i + 1) % count, i)]
    return lax.ppermute(cells, axes, pairs)


def swap_both(near, far, axes, closed):
    far = swap(far, axes, 1, closed)
    return swap(near, axes, 0, closed), far


def local(
    state_field, support_offsets, kernel_values, basis_weight, weight_in, weight_out, cotangent
):
    rows, cols, channels = state_field.shape
    kinds, units = basis_weight.shape[0], weight_in.shape[1]
    grid = state_field.shape
    cells, span = rows * cols, cols + 2 * WIDE
    tall = rows + 2 * RAD
    depth = -(-LAGS * span // LANES) * LANES
    near, far = lax.axis_size(NEAR), lax.axis_size(FAR)
    cot_flat = cotangent.reshape(cells, channels)
    f32, bf16 = jnp.float32, jnp.bfloat16

    odd_lat, odd_lon = lax.axis_index(LAT) % 2, lax.axis_index(LON) % 2
    sides = jnp.stack([odd_lat, odd_lon])
    edge = like((RAD, cols, channels), bf16)
    last = rows - RAD
    to_near = lax.dynamic_slice_in_dim(state_field, jnp.where(odd_lat == 0, last, 0), RAD, 0)
    to_far = lax.dynamic_slice_in_dim(state_field, jnp.where(odd_lat == 0, 0, last), RAD, 0)
    lat_near, lat_far = swap_both(to_near, to_far, LAT, False)

    band_start = lax.axis_index(LAT) * rows
    offsets = lax.dynamic_slice_in_dim(support_offsets, band_start, rows, 0)
    values = lax.dynamic_slice_in_dim(kernel_values, band_start, rows, 1).astype(f32)
    (bands,) = kernel_call(
        functools.partial(bands_kernel, cols),
        (offsets.reshape(rows, -1), values.reshape(kinds, rows, -1)),
        [VMEM, VMEM],
        [like((rows, 2 * kinds * cols, depth), bf16)],
        [pltpu.VMEM((kinds, rows, depth), f32)],
        flops=4 * 10**9,
        name="bands",
    )
    rim = like((tall, WIDE, channels), bf16)
    own = like((rows, WIDE, channels), bf16)
    own_near, own_far = kernel_call(
        inner_edges_kernel, (sides, state_field), [SMEM, VMEM], [own, own], name="inner_edges"
    )
    to_far, to_near = kernel_call(
        edges_kernel,
        (sides, lat_near, lat_far, own_near, own_far),
        [SMEM] + [VMEM] * 4,
        [rim, rim],
        name="edges",
    )
    lon_near, lon_far = swap_both(to_near, to_far, LON, True)
    packed_rows = channels * (2 * units + kinds * channels) // LANES
    core = lax.axis_index(CORE)
    half = like((packed_rows // 2, LANES), bf16)
    packed, hidden, grad_mixed = kernel_call(
        main_kernel,
        (
            sides, bands, lat_near, state_field, lat_far, lon_far, lon_near,
            basis_weight, weight_in, weight_out, cot_flat,
        ),
        [SMEM] + [VMEM] * 10,
        [like((2,) + half.shape, bf16), like((cells, units), bf16), like((cells, channels), bf16)],
        [
            pltpu.VMEM((rows * span + depth, channels), bf16),
            pltpu.VMEM((kinds, cells, channels), bf16),
        ],
        flops=10 * cells * channels * units,
        name="main",
    )

    arrived = swap(packed[1], CORE, 0, True)
    to_far, to_near, middle = kernel_call(
        adjoint_kernel,
        (sides, grad_mixed, basis_weight, bands),
        [SMEM] + [VMEM] * 3,
        [rim, rim, like((tall, cols, channels), f32)],
        [
            pltpu.VMEM((kinds, cells, channels), bf16),
            pltpu.VMEM((rows * span + depth, channels), f32),
        ],
        flops=4 * cells * channels * units,
        name="adjoint",
    )
    chip = kernel_call(
        add_kernel,
        (packed, arrived, to_near),
        [VMEM, VMEM, ANY],
        [half],
        [pltpu.VMEM(half.shape, bf16), pltpu.SemaphoreType.DMA((2,))],
        name="add",
        out_spec=ANY,
    )[0]
    shares = lax.all_to_all(chip.reshape(near, -1, LANES), NEAR, 0, 0)

    near_rim, far_rim = swap_both(to_near, to_far, LON, True)
    planes = sum_and_copy(shares, 1.0, far, near_rim, far_rim)
    planes = lax.all_to_all(planes, FAR, 0, 0)
    to_far, to_near, inside = kernel_call(
        rims_kernel,
        (sides, middle, near_rim, far_rim),
        [SMEM] + [VMEM] * 3,
        [edge, edge, like(grid, f32)],
        name="rims",
    )
    near_edge, far_edge = swap_both(to_near, to_far, LAT, False)
    scale = 1.0 / math.sqrt(cells * lax.axis_size(LAT) * lax.axis_size(LON))
    copies = sum_and_copy(planes, scale, near, near_edge, far_edge)
    block_out, grad_field = kernel_call(
        final_kernel,
        (sides, hidden, weight_out, state_field, cot_flat, inside, near_edge, far_edge),
        [SMEM] + [VMEM] * 7,
        [like(grid, bf16), like(grid, bf16)],
        flops=2 * cells * channels * units,
        name="final",
    )
    mine = lax.all_to_all(copies, NEAR, 0, 0).reshape(-1, LANES)
    other = swap(mine, CORE, 0, True)
    shapes = ((units, channels), (channels, units), (kinds * channels, channels))
    grad_out, grad_in, grad_basis = kernel_call(
        functools.partial(place_kernel, runs_of(shapes, packed_rows // 2)),
        (sides, mine, other),
        [SMEM, VMEM, VMEM],
        [like(shape, bf16) for shape in shapes],
        [*(pltpu.VMEM(shape, bf16) for shape in shapes), pltpu.SemaphoreType.DMA((3,))],
        name="place",
        out_spec=ANY,
    )
    return (block_out, grad_field, grad_basis.reshape(basis_weight.shape), grad_in, grad_out)


def solution(mesh):
    names, sizes = zip(*FINE)
    mesh = Mesh(mesh.devices.reshape(sizes), names)
    return jax.shard_map(
        local,
        mesh=mesh,
        in_specs=(P(LAT, LON, None), P(), P(), P(), P(), P(), P(LAT, LON, None)),
        out_specs=(P(LAT, LON, None), P(LAT, LON, None), P(), P(), P()),
        check_vma=False,
    )
```

```python
import functools
import math

import jax
import jax.numpy as jnp
from jax import lax
from jax.experimental import pallas as pl
from jax.experimental.pallas import tpu as pltpu
from jax.sharding import Mesh
from jax.sharding import PartitionSpec as P

RAD = 2
WIDE = 8
LAGS = 2 * RAD + 1

FINE = (("z_hi", 4), ("x", 4), ("z_mid", 2), ("z_low", 2), ("y", 4), ("core", 2))
LAT = ("z_hi", "x")
LON = ("z_mid", "z_low", "y", "core")
CORE = "core"
NEAR = ("x", "z_low", "y")
FAR = ("z_hi", "z_mid")
LANES = 128
CHUNK = 1024

ROWS, COLS = ((0,), (0,)), ((1,), (1,))
VMEM = pl.BlockSpec(memory_space=pltpu.VMEM)
SMEM = pl.BlockSpec(memory_space=pltpu.SMEM)
ANY = pl.BlockSpec(memory_space=pl.ANY)


def dot(a, b, contract=((1,), (0,))):
    return lax.dot_general(a, b, (contract, ((), ())), preferred_element_type=jnp.float32)


def kernel_call(
    body, operands, specs, outs, scratch=(), flops=0, mib=16, name=None, out_spec=VMEM
):
    moved = sum(x.size * x.dtype.itemsize for x in (*operands, *outs))
    return pl.pallas_call(
        body,
        out_shape=tuple(outs),
        in_specs=specs,
        out_specs=tuple(out_spec for _ in outs),
        scratch_shapes=scratch,
        compiler_params=pltpu.CompilerParams(vmem_limit_bytes=mib << 20),
        cost_estimate=pl.CostEstimate(flops=flops, bytes_accessed=moved, transcendentals=0),
        name=name,
    )(*operands)


def like(shape, dtype):
    return jax.ShapeDtypeStruct(shape, dtype)


def bands_kernel(cols, offset_ref, value_ref, bands_ref, first_ref):
    cycles, height, depth = bands_ref.shape
    kinds, span = height // (2 * cols), cols + 2 * WIDE
    slots = offset_ref.shape[1] // LAGS
    lane = lax.broadcasted_iota(jnp.int32, (cycles, LANES), 1)
    for start in range(0, depth, LANES):
        sums = [jnp.zeros((cycles, LANES), jnp.float32) for _ in range(kinds)]
        for q in range(LAGS):
            if q * span + 2 * WIDE < start or q * span >= start + LANES:
                continue
            for s in range(slots):
                at = slice(q * slots + s, q * slots + s + 1)
                hit = lane == offset_ref[:, at] + (q * span + WIDE - start)
                for k in range(kinds):
                    sums[k] = sums[k] + jnp.where(hit, value_ref[k, :, at], 0.0)
        for k in range(kinds):
            first_ref[k, :, start : start + LANES] = sums[k]
    for i in range(cycles):
        for k in range(kinds):
            block = jnp.broadcast_to(first_ref[k, i : i + 1, :], (cols, depth))
            block = pltpu.roll(block, 0, 1, stride=1, stride_axis=0)
            high = block.astype(jnp.bfloat16)
            low = (block - high.astype(jnp.float32)).astype(jnp.bfloat16)
            bands_ref[i, k * cols : (k + 1) * cols] = high
            bands_ref[i, (kinds + k) * cols : (kinds + k + 1) * cols] = low


def by_side(odd, near, far):
    near, far = near.astype(jnp.float32), far.astype(jnp.float32)
    return jnp.where(odd, near, far), jnp.where(odd, far, near)


def by_partner(odd, before, after):
    near, far = jnp.where(odd, before, after), jnp.where(odd, after, before)
    return near.astype(jnp.bfloat16), far.astype(jnp.bfloat16)


def whole_rows(side_ref, near_ref, state_ref, far_ref):
    above, below = [], []
    for r in range(RAD):
        first, second = by_side(side_ref[0] != 0, near_ref[r], far_ref[r])
        above.append(first)
        below.append(second)
    return above + [state_ref[r].astype(jnp.float32) for r in range(state_ref.shape[0])] + below


def gelu_and_slope(x):
    c, a = math.sqrt(2.0 / math.pi), 0.044715
    square = x * x
    t = jnp.tanh(c * (x + a * (square * x)))
    cdf = 0.5 * (1.0 + t)
    slope = cdf + (0.5 * x) * (1.0 - t * t) * (c * (1.0 + (3.0 * a) * square))
    return x * cdf, slope


def main_kernel(
    side_ref, bands_ref, lat_near_ref, state_ref, lat_far_ref, lon_far_ref, lon_near_ref,
    mix_ref, in_ref, out_ref, cot_ref, packed_ref, hidden_ref, grad_ref, cells_ref, basis_ref,
):
    rows, cols, channels = state_ref.shape
    span = cols + 2 * WIDE
    kinds = basis_ref.shape[0]
    for r, line in enumerate(whole_rows(side_ref, lat_near_ref, state_ref, lat_far_ref)):
        left, right = by_side(side_ref[1] != 0, lon_near_ref[r], lon_far_ref[r])
        line = jnp.concatenate([left, line, right], axis=0)
        cells_ref[r * span : (r + 1) * span] = line.astype(jnp.bfloat16)
    used = (rows + 2 * RAD) * span
    cells_ref[used:] = jnp.zeros((cells_ref.shape[0] - used, channels), jnp.bfloat16)

    depth = bands_ref.shape[2]
    for i in range(rows):
        taken = dot(bands_ref[i], cells_ref[i * span : i * span + depth])
        taken = taken[: kinds * cols] + taken[kinds * cols :]
        for k in range(kinds):
            piece = taken[k * cols : (k + 1) * cols].astype(jnp.bfloat16)
            basis_ref[k, i * cols : (i + 1) * cols] = piece
    mixed = sum(dot(basis_ref[k], mix_ref[k]) for k in range(kinds)).astype(jnp.bfloat16)

    cot = cot_ref[...]
    core, half = side_ref[1], packed_ref.shape[1]

    def pack(matrix, place, height):
        for c in range(0, matrix.shape[1], LANES):
            owner, at = divmod(place + (c // LANES) * height, half)
            slot = core if owner == 0 else 1 - core
            packed_ref[slot, at : at + matrix.shape[0]] = matrix[:, c : c + LANES].astype(jnp.bfloat16)

    units = in_ref.shape[1]
    outer_at, inner_at = 0, units * (channels // LANES)
    basis_at = inner_at + channels * (units // LANES)
    back = jnp.zeros((rows * cols, channels), jnp.float32)
    for c in range(0, units, CHUNK):
        weight = in_ref[:, c : c + CHUNK]
        hidden, slope = gelu_and_slope(dot(mixed, weight))
        hidden = hidden.astype(jnp.bfloat16)
        upstream = dot(cot, out_ref[c : c + CHUNK], COLS)
        grad_pre = (upstream * slope).astype(jnp.bfloat16)
        hidden_ref[:, c : c + CHUNK] = hidden
        back = back + dot(grad_pre, weight, COLS)
        pack(dot(hidden, cot, ROWS), outer_at + c, units)
        pack(dot(mixed, grad_pre, ROWS), inner_at + (c // LANES) * channels, channels)
    grad_mixed = back.astype(jnp.bfloat16)
    grad_ref[...] = grad_mixed
    for k in range(kinds):
        pack(dot(basis_ref[k], grad_mixed, ROWS), basis_at + k * channels, kinds * channels)


def adjoint_kernel(
    side_ref, grad_ref, mix_ref, bands_ref, far_ref, near_ref, middle_ref, back_ref, landing_ref
):
    tall, cols, channels = middle_ref.shape
    rows, span = tall - 2 * RAD, cols + 2 * WIDE
    kinds = mix_ref.shape[0]
    grad = grad_ref[...]
    for k in range(kinds):
        back_ref[k] = dot(grad, mix_ref[k], COLS).astype(jnp.bfloat16)
    landing_ref[...] = jnp.zeros_like(landing_ref)
    depth = bands_ref.shape[2]
    for i in range(rows):
        pieces = [back_ref[k, i * cols : (i + 1) * cols] for k in range(kinds)]
        taken = jnp.concatenate(pieces + pieces, axis=0)
        landing_ref[i * span : i * span + depth] += dot(bands_ref[i], taken, ROWS)
    for r in range(rows + 2 * RAD):
        line = landing_ref[r * span : (r + 1) * span]
        near_ref[r], far_ref[r] = by_partner(side_ref[1] != 0, line[:WIDE], line[WIDE + cols :])
        middle_ref[r] = line[WIDE : WIDE + cols]


def with_rims(side_ref, middle_ref, near_ref, far_ref, r):
    left, right = by_side(side_ref[1] != 0, near_ref[r], far_ref[r])
    line, cols = middle_ref[r], middle_ref.shape[1]
    head, tail = line[:WIDE] + left, line[cols - WIDE :] + right
    return jnp.concatenate([head, line[WIDE : cols - WIDE], tail], axis=0)


def rims_kernel(side_ref, middle_ref, near_ref, far_ref, to_far_ref, to_near_ref):
    rows = middle_ref.shape[0] - 2 * RAD
    for r in range(RAD):
        above = with_rims(side_ref, middle_ref, near_ref, far_ref, r)
        below = with_rims(side_ref, middle_ref, near_ref, far_ref, rows + RAD + r)
        to_near_ref[r], to_far_ref[r] = by_partner(side_ref[0] != 0, above, below)


def final_kernel(
    side_ref, hidden_ref, out_ref, state_ref, cot_ref, middle_ref, near_rim_ref, far_rim_ref,
    near_ref, far_ref, block_ref, field_ref,
):
    rows, cols = state_ref.shape[:2]
    branch = dot(hidden_ref[...], out_ref[...])
    rims = (side_ref, middle_ref, near_rim_ref, far_rim_ref)
    lines = [with_rims(*rims, RAD + r) for r in range(rows)]
    for r in range(RAD):
        above, below = by_side(side_ref[0] != 0, near_ref[r], far_ref[r])
        lines[r] = lines[r] + above
        lines[rows - RAD + r] = lines[rows - RAD + r] + below
    for r in range(rows):
        at = slice(r * cols, (r + 1) * cols)
        block_ref[r] = (state_ref[r].astype(jnp.float32) + branch[at]).astype(jnp.bfloat16)
        field_ref[r] = (cot_ref[at].astype(jnp.float32) + lines[r]).astype(jnp.bfloat16)


def inner_edges_kernel(side_ref, state_ref, near_ref, far_ref):
    rows, cols = state_ref.shape[:2]
    for r in range(rows):
        line = state_ref[r].astype(jnp.float32)
        near_ref[r], far_ref[r] = by_partner(side_ref[1] != 0, line[:WIDE], line[cols - WIDE :])


def edges_kernel(side_ref, lat_near_ref, lat_far_ref, own_near_ref, own_far_ref, far_ref, near_ref):
    rows, cols = own_near_ref.shape[0], lat_near_ref.shape[1]
    near_ref[RAD : RAD + rows] = own_near_ref[...]
    far_ref[RAD : RAD + rows] = own_far_ref[...]
    for r in range(RAD):
        lines = by_side(side_ref[0] != 0, lat_near_ref[r], lat_far_ref[r])
        for at, line in zip((r, RAD + rows + r), lines):
            near_ref[at], far_ref[at] = by_partner(side_ref[1] != 0, line[:WIDE], line[cols - WIDE :])


def add_kernel(a_ref, b_ref, later_than_ref, sum_hbm, sum_ref, sems):
    pieces = sems.shape[0]
    height = sum_ref.shape[0] // pieces
    copies = []
    for i in range(pieces):
        at = slice(i * height, (i + 1) * height)
        total = a_ref[0, at].astype(jnp.float32) + b_ref[at].astype(jnp.float32)
        sum_ref[at] = total.astype(jnp.bfloat16)
        span = pl.ds(i * height, height)
        copies.append(pltpu.make_async_copy(sum_ref.at[span], sum_hbm.at[span], sems.at[i]))
        copies[i].start()
    for copy in copies:
        copy.wait()


def tie_kernel(value_ref, *refs):
    refs[-1][...] = value_ref[...]


def tie(value, *later_than):
    return kernel_call(
        tie_kernel,
        (value, *later_than),
        [VMEM] + [ANY] * len(later_than),
        [like(value.shape, value.dtype)],
        name="tie",
    )[0]


def sum_kernel(scale, parts_ref, *refs):
    out_ref = refs[-1]
    total = parts_ref[0].astype(jnp.float32)
    for i in range(1, parts_ref.shape[0]):
        total = total + parts_ref[i].astype(jnp.float32)
    total = (total * scale).astype(out_ref.dtype)
    for i in range(out_ref.shape[0]):
        out_ref[i] = total


def sum_and_copy(parts, scale, copies, *later_than):
    return kernel_call(
        functools.partial(sum_kernel, scale),
        (parts, *later_than),
        [VMEM] + [ANY] * len(later_than),
        [like((copies,) + parts.shape[1:], jnp.bfloat16)],
        flops=parts.size,
        mib=16,
        name="sum_and_copy",
    )[0]


def runs_of(shapes, half):
    runs, start = ([], []), 0
    for out, (rows, cols) in enumerate(shapes):
        for col in range(0, cols, LANES):
            at = start
            while at < start + rows:
                which = at // half
                height = min(start + rows, (which + 1) * half) - at
                runs[which].append((out, at - start, col, at - which * half, height))
                at += height
            start += rows
    return runs


def place_kernel(runs, side_ref, mine_ref, other_ref, *refs):
    *refs, sems = refs
    count = len(refs) // 2
    outs, places = refs[:count], refs[count:]
    copies = []
    for o, place_ref in enumerate(places):
        for core in range(2):

            @pl.when(side_ref[1] == core)
            def _(core=core, o=o, place_ref=place_ref):
                for which in range(2):
                    half_ref = mine_ref if which == core else other_ref
                    for out, row, col, at, height in runs[which]:
                        if out == o:
                            place_ref[row : row + height, col : col + LANES] = half_ref[at : at + height]

        copies.append(pltpu.make_async_copy(place_ref, outs[o], sems.at[o]))
        copies[o].start()
    for copy in copies:
        copy.wait()


def swap(cells, axes, lead, closed):
    count = lax.axis_size(axes)
    pairs = []
    for i in range(lead, count, 2):
        if closed or i + 1 < count:
            pairs += [(i, (i + 1) % count), ((i + 1) % count, i)]
    return lax.ppermute(cells, axes, pairs)


def swap_both(near, far, axes, closed):
    far = swap(far, axes, 1, closed)
    return swap(near, axes, 0, closed), far


def local(
    state_field, support_offsets, kernel_values, basis_weight, weight_in, weight_out, cotangent
):
    rows, cols, channels = state_field.shape
    kinds, units = basis_weight.shape[0], weight_in.shape[1]
    grid = state_field.shape
    cells, span = rows * cols, cols + 2 * WIDE
    tall = rows + 2 * RAD
    depth = -(-LAGS * span // LANES) * LANES
    near, far = lax.axis_size(NEAR), lax.axis_size(FAR)
    cot_flat = cotangent.reshape(cells, channels)
    f32, bf16 = jnp.float32, jnp.bfloat16

    odd_lat, odd_lon = lax.axis_index(LAT) % 2, lax.axis_index(LON) % 2
    sides = jnp.stack([odd_lat, odd_lon])
    edge = like((RAD, cols, channels), bf16)
    last = rows - RAD
    to_near = lax.dynamic_slice_in_dim(state_field, jnp.where(odd_lat == 0, last, 0), RAD, 0)
    to_far = lax.dynamic_slice_in_dim(state_field, jnp.where(odd_lat == 0, 0, last), RAD, 0)
    lat_near, lat_far = swap_both(to_near, to_far, LAT, False)

    band_start = lax.axis_index(LAT) * rows
    offsets = lax.dynamic_slice_in_dim(support_offsets, band_start, rows, 0)
    values = lax.dynamic_slice_in_dim(kernel_values, band_start, rows, 1).astype(f32)
    (bands,) = kernel_call(
        functools.partial(bands_kernel, cols),
        (offsets.reshape(rows, -1), values.reshape(kinds, rows, -1)),
        [VMEM, VMEM],
        [like((rows, 2 * kinds * cols, depth), bf16)],
        [pltpu.VMEM((kinds, rows, depth), f32)],
        flops=4 * 10**9,
        name="bands",
    )
    rim = like((tall, WIDE, channels), bf16)
    own = like((rows, WIDE, channels), bf16)
    own_near, own_far = kernel_call(
        inner_edges_kernel, (sides, state_field), [SMEM, VMEM], [own, own], name="inner_edges"
    )
    to_far, to_near = kernel_call(
        edges_kernel,
        (sides, lat_near, lat_far, own_near, own_far),
        [SMEM] + [VMEM] * 4,
        [rim, rim],
        name="edges",
    )
    lon_near, lon_far = swap_both(to_near, to_far, LON, True)
    packed_rows = channels * (2 * units + kinds * channels) // LANES
    core = lax.axis_index(CORE)
    half = like((packed_rows // 2, LANES), bf16)
    packed, hidden, grad_mixed = kernel_call(
        main_kernel,
        (
            sides, bands, lat_near, state_field, lat_far, lon_far, lon_near,
            basis_weight, weight_in, weight_out, cot_flat,
        ),
        [SMEM] + [VMEM] * 10,
        [like((2,) + half.shape, bf16), like((cells, units), bf16), like((cells, channels), bf16)],
        [
            pltpu.VMEM((rows * span + depth, channels), bf16),
            pltpu.VMEM((kinds, cells, channels), bf16),
        ],
        flops=10 * cells * channels * units,
        name="main",
    )

    arrived = swap(packed[1], CORE, 0, True)
    to_far, to_near, middle = kernel_call(
        adjoint_kernel,
        (sides, grad_mixed, basis_weight, bands),
        [SMEM] + [VMEM] * 3,
        [rim, rim, like((tall, cols, channels), f32)],
        [
            pltpu.VMEM((kinds, cells, channels), bf16),
            pltpu.VMEM((rows * span + depth, channels), f32),
        ],
        flops=4 * cells * channels * units,
        name="adjoint",
    )
    chip = kernel_call(
        add_kernel,
        (packed, arrived, to_near),
        [VMEM, VMEM, ANY],
        [half],
        [pltpu.VMEM(half.shape, bf16), pltpu.SemaphoreType.DMA((4,))],
        name="add",
        out_spec=ANY,
    )[0]
    shares = lax.all_to_all(chip.reshape(near, -1, LANES), NEAR, 0, 0)

    near_rim, far_rim = swap_both(to_near, to_far, LON, True)
    planes = sum_and_copy(shares, 1.0, far, near_rim, far_rim)
    planes = lax.all_to_all(planes, FAR, 0, 0)
    to_far, to_near = kernel_call(
        rims_kernel,
        (sides, middle, near_rim, far_rim),
        [SMEM] + [VMEM] * 3,
        [edge, edge],
        name="rims",
    )
    near_edge, far_edge = swap_both(to_near, to_far, LAT, False)
    scale = 1.0 / math.sqrt(cells * lax.axis_size(LAT) * lax.axis_size(LON))
    copies = sum_and_copy(planes, scale, near, near_edge, far_edge)
    block_out, grad_field = kernel_call(
        final_kernel,
        (sides, hidden, weight_out, state_field, cot_flat, middle, near_rim, far_rim, near_edge, far_edge),
        [SMEM] + [VMEM] * 9,
        [like(grid, bf16), like(grid, bf16)],
        flops=2 * cells * channels * units,
        name="final",
    )
    mine = lax.all_to_all(copies, NEAR, 0, 0).reshape(-1, LANES)
    other = swap(mine, CORE, 0, True)
    shapes = ((units, channels), (channels, units), (kinds * channels, channels))
    grad_out, grad_in, grad_basis = kernel_call(
        functools.partial(place_kernel, runs_of(shapes, packed_rows // 2)),
        (sides, mine, other),
        [SMEM, VMEM, VMEM],
        [like(shape, bf16) for shape in shapes],
        [*(pltpu.VMEM(shape, bf16) for shape in shapes), pltpu.SemaphoreType.DMA((3,))],
        name="place",
        out_spec=ANY,
    )
    return (block_out, grad_field, grad_basis.reshape(basis_weight.shape), grad_in, grad_out)


def solution(mesh):
    names, sizes = zip(*FINE)
    mesh = Mesh(mesh.devices.reshape(sizes), names)
    return jax.shard_map(
        local,
        mesh=mesh,
        in_specs=(P(LAT, LON, None), P(), P(), P(), P(), P(), P(LAT, LON, None)),
        out_specs=(P(LAT, LON, None), P(LAT, LON, None), P(), P(), P()),
        check_vma=False,
    )
```
